512 devices in a mesh: gz: 16 (over y, core), gy: 32 (over x, z).
Axes of the slice: x: 4, y: 8, z: 8, core: 2. Of those that a mesh axis runs over, the one named last changes fastest.
Arguments:
- field: bfloat16 [8, 512, 64, 2048], P(None, 'gy', None, 'gz'), may hold values from -6 to 6
- spectral_weight: bfloat16 [64, 32, 2, 64, 64], P('gy', None, None, 'gz'), may hold values from -4 to 4
- local_weight: bfloat16 [64, 64], replicated, may hold values from -0.75 to 0.75
- bias: bfloat16 [64], replicated, may hold values from -3 to 3
Outputs:
- mixed: bfloat16 [8, 512, 64, 2048], P(None, 'gy', None, 'gz')
The draws below stay inside these ranges and needn't reach their ends.
All inputs are finite; a program needn't handle non-finite values.
Results may differ from the reference program's by a relative error of at most 0.017.
Values may be sent and summed in bfloat16 or wider, within the bound.
A program may use at most 64 MiB of HBM per device.

```python
import math
import jax
import jax.numpy as jnp
from jax import lax

NX = 8
C = 64
MY = 32
MZ = 32
CY = 16
CZ = 128
KY = 64
NY = 512
NZ = 2048


def shard_levels(key, extent, pieces, low, high):
    def one(dim, blocks):
        draws = jax.random.uniform(jax.random.fold_in(jax.random.fold_in(key, 6), dim), (blocks,), jnp.float32, low / len(pieces), high / len(pieces))
        return jnp.repeat(jnp.exp(draws), extent[dim] // blocks).reshape((-1,) + (1,) * (len(extent) - dim - 1))

    loudness = one(*pieces[0])
    for cut in pieces[1:]:
        loudness = loudness * one(*cut)
    return loudness


def centred(stream_key, dims, scale, limit, pieces=(), kind=jnp.bfloat16):
    gain = shard_levels(stream_key, dims, pieces, -0.22, 0.18) if pieces else 1.0
    array = jax.random.normal(stream_key, dims, jnp.float32) * scale * gain
    return jnp.minimum(jnp.maximum(array, -limit), limit).astype(kind)


def setup_inputs(seed: int = 0) -> dict:
    seeds = jax.random.split(jax.random.key(seed), 5)
    field = centred(seeds[0], (NX, NY, C, NZ), 1.0, 6.0, ((1, 32), (3, 16)))
    spectral_weight = centred(seeds[1], (KY, MZ, 2, C, C), (max(1, 16 * C * KY * MZ // (NY * NZ))) ** -0.5, 4.0, ((0, 32), (3, 16)))
    local_weight = centred(seeds[2], (C, C), C ** -0.5, 0.75)
    bias = centred(seeds[3], (C,), 0.5, 3.0)
    return dict(field=field, spectral_weight=spectral_weight, local_weight=local_weight, bias=bias)


def phase_of(first, second, modulus):
    return ((first * second) % modulus).astype(jnp.float32) * (2.0 * math.pi / modulus)


def gelu_tanh(value):
    return 0.5 * value * (1.0 + jnp.tanh(0.7978845608 * (value + 0.044715 * value * value * value)))


def reference(field, spectral_weight, local_weight, bias):
    highest = lax.Precision.HIGHEST
    z_store = jnp.arange(NZ, dtype=jnp.int32)
    z_coords = ((z_store % CZ) * (NZ // CZ) + z_store // CZ).astype(jnp.int32)
    y_store = jnp.arange(NY, dtype=jnp.int32)
    y_coords = ((y_store % CY) * (NY // CY) + y_store // CY).astype(jnp.int32)
    kz_index = jnp.arange(MZ, dtype=jnp.int32)
    z_phase = phase_of(z_coords[:, None], kz_index[None, :], NZ)
    z_table = jnp.stack([jnp.cos(z_phase), -jnp.sin(z_phase)], -1).astype(jnp.bfloat16).astype(jnp.float32)
    ky_index = jnp.arange(KY, dtype=jnp.int32)
    wavenum = jnp.where(ky_index < MY, ky_index, ky_index + NY - 2 * MY).astype(jnp.int32)
    y_phase = phase_of(wavenum[:, None], y_coords[None, :], NY)
    y_cosine = jnp.cos(y_phase).astype(jnp.bfloat16).astype(jnp.float32)
    y_sine = jnp.sin(y_phase).astype(jnp.bfloat16).astype(jnp.float32)
    doubling = jnp.where(kz_index == 0, 1.0, 2.0).astype(jnp.float32)
    back_phase = phase_of(kz_index[:, None], z_coords[None, :], NZ)
    back_table = jnp.stack([doubling[:, None] * jnp.cos(back_phase), -(doubling[:, None] * jnp.sin(back_phase))], 1)
    back_table = back_table.astype(jnp.bfloat16).astype(jnp.float32)
    weight_real = spectral_weight[:, :, 0].astype(jnp.float32)
    weight_imag = spectral_weight[:, :, 1].astype(jnp.float32)
    pointwise = local_weight.astype(jnp.float32)
    offset = bias.astype(jnp.float32)

    def plane(layer):
        values = layer.astype(jnp.float32)
        zmodes = jnp.einsum('ycz,zkp->kpyc', values, z_table, precision=highest)
        z_real, z_imag = zmodes[:, 0], zmodes[:, 1]
        spec_real = jnp.einsum('jy,kyc->jkc', y_cosine, z_real, precision=highest) + jnp.einsum('jy,kyc->jkc', y_sine, z_imag, precision=highest)
        spec_imag = jnp.einsum('jy,kyc->jkc', y_cosine, z_imag, precision=highest) - jnp.einsum('jy,kyc->jkc', y_sine, z_real, precision=highest)
        prod_real = jnp.einsum('jkc,jkco->jko', spec_real, weight_real, precision=highest) - jnp.einsum('jkc,jkco->jko', spec_imag, weight_imag, precision=highest)
        prod_imag = jnp.einsum('jkc,jkco->jko', spec_real, weight_imag, precision=highest) + jnp.einsum('jkc,jkco->jko', spec_imag, weight_real, precision=highest)
        prod_real = lax.optimization_barrier(prod_real.astype(jnp.bfloat16)).astype(jnp.float32)
        prod_imag = lax.optimization_barrier(prod_imag.astype(jnp.bfloat16)).astype(jnp.float32)
        rows_real = jnp.einsum('jy,jko->kyo', y_cosine, prod_real, precision=highest) - jnp.einsum('jy,jko->kyo', y_sine, prod_imag, precision=highest)
        rows_imag = jnp.einsum('jy,jko->kyo', y_sine, prod_real, precision=highest) + jnp.einsum('jy,jko->kyo', y_cosine, prod_imag, precision=highest)
        rows_pair = jnp.stack([rows_real, rows_imag], 1)
        rows_pair = lax.optimization_barrier(rows_pair.astype(jnp.bfloat16)).astype(jnp.float32)
        spectral = jnp.einsum('kpz,kpyc->ycz', back_table, rows_pair, precision=highest) / float(NY * NZ)
        linear = jnp.einsum('oc,ycz->yoz', pointwise, values, precision=highest)
        return gelu_tanh(spectral + linear + offset[None, :, None]).astype(jnp.bfloat16)

    return lax.map(plane, field)
```

```python
import functools
import math

import jax
import jax.numpy as jnp
import ml_dtypes
import numpy as np
from jax import lax
from jax.experimental import pallas as pl
from jax.experimental.pallas import tpu as pltpu
from jax.sharding import PartitionSpec as P

MESH = pl.DeviceIdType.MESH
BF16 = jnp.bfloat16
F32 = jnp.float32
CHUNKS = 2


def phase_of(number, modulus):
    return (number % modulus).astype(np.float32) * np.float32(2.0 * math.pi / modulus)


def rounded(array):
    return np.asarray(array, np.float32).astype(ml_dtypes.bfloat16).astype(np.float32)


def z_tables(ring, depth):
    size = 2 * ring
    cell = np.arange(depth)
    tables = []
    for d in range(size):
        owner = np.array(
            [((d // 2 + t) % ring) * 2 + (d % 2 ^ r) for r in range(2) for t in range(ring)]
        )
        mode = owner[:, None] * 2 + np.arange(2)
        angle = phase_of(mode[:, :, None] * (cell * size + d), depth * size)
        base = np.stack([np.cos(angle), -np.sin(angle)], 2)
        tables.append(np.repeat(base[:, None], 4, 1).reshape(size * 16, depth))
    return rounded(np.stack(tables))


def y_tables(nx, nz, rows):
    size = nx * nz
    total = rows * size
    forward, back = [], []
    for e in range(size):
        owner = np.array(
            [((e // nz + a) % nx) * nz + (e % nz + b) % nz for a in range(nx) for b in range(nz)]
        )
        mode = owner[:, None] * 2 + np.arange(2)
        wave = np.where(mode < size, mode, mode + total - 2 * size)
        angle = phase_of(wave[:, :, None] * (np.arange(rows) * size + e), total)
        cosine, sine = np.cos(angle), np.sin(angle)
        there = np.stack([np.stack([cosine, sine], -1), np.stack([-sine, cosine], -1)], 2)
        there = np.einsum("ujqyp,kl->ujkqylp", there, np.eye(2))
        forward.append(there.reshape(size * 8, rows * 4))
        here = np.stack([np.stack([cosine, -sine], -1), np.stack([sine, cosine], -1)], 2)
        here = np.einsum("ujqyp,kl->ykqujlp", here, np.eye(2))
        back.append(here.reshape(rows * 4, size * 8))
    return rounded(np.stack(forward)), rounded(np.stack(back))


def gelu_tanh(value):
    return 0.5 * value * (1.0 + jnp.tanh(0.7978845608 * (value + 0.044715 * value * value * value)))


def split(value):
    high = value.astype(BF16)
    return high, (value - high.astype(F32)).astype(BF16)


def dot(left, right, dims=((1,), (0,))):
    return lax.dot_general(left, right, (dims, ((), ())), preferred_element_type=F32)


def kernel(
    geometry, scale,
    field, weight, pointwise, bias, table_z, table_f, table_b, out,
    fv, wv, tz, tf, tb, acc, sib_out, sib_in, a_out, a_in, b_out, b_in, c_in, d_in,
    w_mess, w_out, w_in, w_stage, w_full, small, wide, lin,
    local, local_f, local_w, sib_s, sib_r, a_s, a_r, b_s, b_r, c_s, c_r, d_s, d_r, e_s, e_r, w_s, w_r,
):
    ring, nx, nz, planes, rows, channels, depth = geometry
    gz, gy = 2 * ring, nx * nz
    per = planes // CHUNKS
    lanes = per * channels
    half = lanes // 2
    groups = rows // 4
    band = channels // gz
    d = lax.axis_index("gz")
    e = lax.axis_index("gy")
    core = lax.rem(d, 2)

    def chip(t):
        return {"gz": lax.rem(d + 2 * t, gz)}

    sibling = {"gz": d + 1 - 2 * core}
    ex, ez = e // nz, lax.rem(e, nz)

    def plane(a, b):
        return {"gy": lax.rem(ex + a, nx) * nz + lax.rem(ez + b, nz)}

    partners = [(a, b) for a in range(nx) for b in range(nz)][1:]

    def slot(a, b):
        return ((nx - a) % nx) * nz + (nz - b) % nz

    def remote(src, dst, send, recv, device):
        return pltpu.make_async_remote_copy(
            src_ref=src, dst_ref=dst, send_sem=send, recv_sem=recv, device_id=device, device_id_type=MESH
        )

    get_tz = pltpu.make_async_copy(table_z.at[d], tz, local.at[0])
    get_f = [
        pltpu.make_async_copy(
            field.at[pl.ds(ch * per, per)], fv.at[pl.ds(ch * per, per)], local_f.at[ch]
        )
        for ch in range(CHUNKS)
    ]
    get_w = pltpu.make_async_copy(weight, wv, local.at[1])
    get_tf = pltpu.make_async_copy(table_f.at[e], tf, local.at[2])
    get_tb = pltpu.make_async_copy(table_b.at[e], tb, local.at[3])
    get_tz.start()
    for copy in get_f:
        copy.start()
    get_w.start()
    get_tf.start()
    get_tb.start()

    barrier = pltpu.get_barrier_semaphore()
    for step in range(1, gz):
        pl.semaphore_signal(
            barrier, inc=1, device_id={"gz": lax.rem(d + step, gz)}, device_id_type=MESH
        )
    for a, b in partners:
        pl.semaphore_signal(barrier, inc=1, device_id=plane(a, b), device_id_type=MESH)
    pl.semaphore_wait(barrier, gz - 1 + gy - 1)

    get_tz.wait()
    member = lax.rem(lax.broadcasted_iota(jnp.int32, (gz * 16, depth), 0) // 4, 4)
    table = jnp.concatenate(
        [jnp.where(member == i, tz[...], 0.0).astype(BF16) for i in range(4)], axis=1
    )
    own_rows = ring * 16
    for ch in range(CHUNKS):
        get_f[ch].wait()
        for g in range(groups):
            cells = jnp.concatenate(
                [
                    fv[ch * per : (ch + 1) * per, g * 4 + i].reshape(lanes, depth)
                    for i in range(4)
                ],
                axis=1,
            )
            part = dot(table, cells, ((1,), (1,)))
            sib_out[ch, g] = part[own_rows:].astype(BF16)
            acc[ch, g] = part[:own_rows]
            remote(
                sib_out.at[ch, g], sib_in.at[ch, g], sib_s.at[ch, g], sib_r.at[ch, g], sibling
            ).start()

    for ch in range(CHUNKS):
        for g in range(groups):
            remote(
                sib_out.at[ch, g], sib_in.at[ch, g], sib_s.at[ch, g], sib_r.at[ch, g], sibling
            ).wait_recv()
            total = acc[ch, g] + sib_in[ch, g].astype(F32)
            acc[ch, g, 0:16] = total[0:16]
            for t in range(1, ring):
                a_out[ch, t - 1, g * 16 : (g + 1) * 16] = total[t * 16 : (t + 1) * 16].astype(BF16)
        for t in range(1, ring):
            remote(
                a_out.at[ch, t - 1], a_in.at[ch, ring - 1 - t], a_s.at[ch], a_r.at[ch], chip(t)
            ).start()

    get_w.wait()
    for jj in range(2):
        for k in range(2 * gz):
            for p in range(2):
                row = (jj * 2 + k % 2) * band
                w_mess[k // 2, row : row + band, p * channels : (p + 1) * channels] = wv[
                    jj, k, p
                ].astype(F32)
    w_out[...] = w_mess[...].astype(BF16)
    own_w = pltpu.make_async_copy(w_out.at[d], w_in.at[d], local_w)
    own_w.start()
    for step in range(1, gz):
        dest = lax.rem(d + step, gz)
        remote(w_out.at[dest], w_in.at[d], w_s, w_r, {"gz": dest}).start()

    block = per * channels
    row_id = lax.broadcasted_iota(jnp.int32, (block, block), 0) // channels
    col_id = lax.broadcasted_iota(jnp.int32, (block, block), 1) // channels
    row = jnp.concatenate([pointwise[...].astype(F32)] * per, axis=1)
    mixing = jnp.where(row_id == col_id, jnp.concatenate([row] * per, axis=0), 0.0).astype(BF16)
    first = lax.broadcasted_iota(jnp.int32, (block, channels), 0)
    second = lax.broadcasted_iota(jnp.int32, (block, channels), 1)
    pick = jnp.where(
        lax.rem(first, channels) == second, jnp.broadcast_to(bias[...].astype(F32), (block, channels)), 0.0
    ).astype(BF16)
    offset = dot(pick, jnp.ones((channels, 4 * depth), BF16))
    for ch in range(CHUNKS):
        for g in range(groups):
            cells = jnp.concatenate(
                [
                    fv[ch * per : (ch + 1) * per, g * 4 + i].reshape(lanes, depth)
                    for i in range(4)
                ],
                axis=1,
            )
            lin[ch, g] = dot(mixing, cells) + offset

    get_tf.wait()
    ahead = tf[...].astype(BF16)
    ahead = jnp.concatenate([ahead, ahead], axis=1)
    for ch in range(CHUNKS):
        remote(a_in.at[ch], a_in.at[ch], a_s.at[ch], a_r.at[ch], chip(1)).wait_recv()
        modes = jnp.concatenate([acc[ch, g, 0:16] for g in range(groups)], axis=0)
        for t in range(ring - 1):
            modes = modes + a_in[ch, t].astype(F32)
        high, low = split(modes)
        part = dot(ahead, jnp.concatenate([high, low], axis=0))
        part = part.reshape(gy, 8, lanes)
        b_out[ch] = jnp.concatenate([part[:, :, :half], part[:, :, half:]], axis=1).astype(BF16)
        b_in[ch, 0] = b_out[ch, 0]
        for a, b in partners:
            remote(
                b_out.at[ch, a * nz + b], b_in.at[ch, slot(a, b)], b_s.at[ch], b_r.at[ch], plane(a, b)
            ).start()

    own_w.wait()
    remote(w_in.at[pl.ds(0, gz - 1)], w_in.at[pl.ds(0, gz - 1)], w_s, w_r, chip(1)).wait_recv()
    w_mess[...] = w_in[...].astype(F32)
    for source in range(gz):
        for jk in range(4):
            w_stage[jk, source * band : (source + 1) * band] = w_mess[
                source, jk * band : (jk + 1) * band
            ]
    sign = jnp.where(
        lax.broadcasted_iota(jnp.int32, (channels, 2 * channels), 1) < channels, -1.0, 1.0
    )
    for jk in range(4):
        upper = w_stage[jk]
        lower = pltpu.roll(upper, channels, 1) * sign
        w_full[jk] = jnp.concatenate([upper, lower], axis=0).astype(BF16)

    per_half = per // 2
    for ch in range(CHUNKS):
        remote(
            b_in.at[ch, pl.ds(1, gy - 1)], b_in.at[ch, pl.ds(1, gy - 1)], b_s.at[ch], b_r.at[ch], plane(0, 1)
        ).wait_recv()
        spectrum = jnp.sum(b_in[ch].astype(F32), axis=0)
        for h in range(half // 128):
            small[h] = spectrum[:, h * 128 : (h + 1) * 128]
        for h in range(half // 128):
            real = small[h, pl.ds(0, 8, stride=2), :]
            imag = small[h, pl.ds(1, 8, stride=2), :]
            for s in range(128 // channels):
                lane = s * channels
                x = h * (128 // channels) + s
                wide[x * 8 : (x + 1) * 8, :] = jnp.concatenate(
                    [real[:, lane : lane + channels], imag[:, lane : lane + channels]], axis=1
                )
        products = []
        for jk in range(4):
            high, low = split(wide[pl.ds(jk, 2 * per_half, stride=4), :])
            both = dot(jnp.concatenate([high, low], axis=0), w_full[jk])
            products.append(both[: 2 * per_half] + both[2 * per_half :])
        for jk in range(4):
            wide[pl.ds(jk, 2 * per_half, stride=4), :] = products[jk]
        for h in range(half // 128):
            pieces = [
                wide[(h * (128 // channels) + s) * 8 : (h * (128 // channels) + s + 1) * 8, :]
                for s in range(128 // channels)
            ]
            small[h, pl.ds(0, 8, stride=2), :] = jnp.concatenate(
                [piece[:, :channels] for piece in pieces], axis=1
            )
            small[h, pl.ds(1, 8, stride=2), :] = jnp.concatenate(
                [piece[:, channels:] for piece in pieces], axis=1
            )
        c_in[ch, 0] = jnp.concatenate([small[h] for h in range(half // 128)], axis=1).astype(BF16)
        for a, b in partners:
            remote(
                c_in.at[ch, 0], c_in.at[ch, slot(a, b)], c_s.at[ch], c_r.at[ch], plane(a, b)
            ).start()

    get_tb.wait()
    behind = tb[...].astype(BF16)
    line = lax.broadcasted_iota(jnp.int32, (rows * 4, lanes), 0)
    low_mode = jnp.logical_and(lax.rem(line, 4) < 2, d == 0)
    factor = jnp.where(low_mode, scale, 2.0 * scale)
    for ch in range(CHUNKS):
        remote(
            c_in.at[ch, pl.ds(1, gy - 1)], c_in.at[ch, pl.ds(1, gy - 1)], c_s.at[ch], c_r.at[ch], plane(0, 1)
        ).wait_recv()
        bands = c_in[ch].astype(F32)
        bands = jnp.concatenate([bands[:, 0:8], bands[:, 8:16]], axis=2)
        bands = bands.reshape(gy * 8, lanes).astype(BF16)
        d_in[ch, 0, 0] = (dot(behind, bands) * factor).astype(BF16)
        remote(d_in.at[ch, 0, 0], d_in.at[ch, 1, 0], e_s.at[ch, 0], e_r.at[ch, 0], sibling).start()
        for t in range(1, ring):
            remote(
                d_in.at[ch, 0, 0], d_in.at[ch, 0, ring - t], d_s.at[ch], d_r.at[ch, ring - t], chip(t)
            ).start()

    order = sorted(range(1, ring), key=lambda t: min(t, ring - t))
    for ch in range(CHUNKS):
        for t in order:
            remote(
                d_in.at[ch, 0, 0], d_in.at[ch, 0, t], d_s.at[ch], d_r.at[ch, t], chip(1)
            ).wait_recv()
            remote(
                d_in.at[ch, 0, t], d_in.at[ch, 1, t], e_s.at[ch, t], e_r.at[ch, t], sibling
            ).start()
        for t in [0] + order:
            remote(
                d_in.at[ch, 0, t], d_in.at[ch, 1, t], e_s.at[ch, t], e_r.at[ch, t], sibling
            ).wait_recv()
        for g in range(groups):
            spectral = d_in[ch, :, :, g * 16 : (g + 1) * 16].reshape(gz * 16, lanes)
            value = gelu_tanh(dot(spectral, table, ((0,), (0,))) + lin[ch, g])
            value = value.astype(BF16).reshape(per, channels, 4 * depth)
            for i in range(4):
                out[ch * per : (ch + 1) * per, g * 4 + i] = value[:, :, i * depth : (i + 1) * depth]

    for ch in range(CHUNKS):
        for g in range(groups):
            remote(
                sib_out.at[ch, g], sib_in.at[ch, g], sib_s.at[ch, g], sib_r.at[ch, g], sibling
            ).wait_send()
        remote(a_out.at[ch], a_in.at[ch], a_s.at[ch], a_r.at[ch], chip(1)).wait_send()
        remote(
            b_out.at[ch, pl.ds(1, gy - 1)], b_in.at[ch, pl.ds(1, gy - 1)], b_s.at[ch], b_r.at[ch], plane(0, 1)
        ).wait_send()
        remote(
            c_in.at[ch, pl.ds(1, gy - 1)], c_in.at[ch, pl.ds(1, gy - 1)], c_s.at[ch], c_r.at[ch], plane(0, 1)
        ).wait_send()
        remote(
            d_in.at[ch, 0, pl.ds(1, ring - 1)], d_in.at[ch, 0, pl.ds(1, ring - 1)], d_s.at[ch], d_r.at[ch, 1], chip(1)
        ).wait_send()
        for t in range(ring):
            remote(
                d_in.at[ch, 0, t], d_in.at[ch, 1, t], e_s.at[ch, t], e_r.at[ch, t], sibling
            ).wait_send()
    remote(w_in.at[pl.ds(0, gz - 1)], w_in.at[pl.ds(0, gz - 1)], w_s, w_r, chip(1)).wait_send()


def on_device(ring, nx, nz, field, spectral_weight, local_weight, bias):
    planes, rows, channels, depth = field.shape
    gz, gy = 2 * ring, nx * nz
    geometry = (ring, nx, nz, planes, rows, channels, depth)
    scale = 1.0 / (rows * gy * depth * gz)
    forward, back = y_tables(nx, nz, rows)
    table_z = z_tables(ring, depth)
    per = planes // CHUNKS
    lanes = per * channels
    half = lanes // 2
    groups = rows // 4
    band = channels // gz
    dma = pltpu.SemaphoreType.DMA
    scratch = [
        pltpu.VMEM(field.shape, BF16),
        pltpu.VMEM(spectral_weight.shape, BF16),
        pltpu.VMEM(table_z.shape[1:], F32),
        pltpu.VMEM(forward.shape[1:], F32),
        pltpu.VMEM(back.shape[1:], F32),
        pltpu.VMEM((CHUNKS, groups, ring * 16, lanes), F32),
        pltpu.VMEM((CHUNKS, groups, ring * 16, lanes), BF16),
        pltpu.VMEM((CHUNKS, groups, ring * 16, lanes), BF16),
        pltpu.VMEM((CHUNKS, ring - 1, rows * 4, lanes), BF16),
        pltpu.VMEM((CHUNKS, ring - 1, rows * 4, lanes), BF16),
        pltpu.VMEM((CHUNKS, gy, 16, half), BF16),
        pltpu.VMEM((CHUNKS, gy, 16, half), BF16),
        pltpu.VMEM((CHUNKS, gy, 16, half), BF16),
        pltpu.VMEM((CHUNKS, 2, ring, rows * 4, lanes), BF16),
        pltpu.VMEM((gz, 4 * band, 2 * channels), F32),
        pltpu.VMEM((gz, 4 * band, 2 * channels), BF16),
        pltpu.VMEM((gz, 4 * band, 2 * channels), BF16),
        pltpu.VMEM((4, channels, 2 * channels), F32),
        pltpu.VMEM((4, 2 * channels, 2 * channels), BF16),
        pltpu.VMEM((half // 128, 16, 128), F32),
        pltpu.VMEM((per * 4, 2 * channels), F32),
        pltpu.VMEM((CHUNKS, groups, lanes, 4 * depth), F32),
        dma((4,)), dma((CHUNKS,)), dma,
        dma((CHUNKS, groups)), dma((CHUNKS, groups)),
        dma((CHUNKS,)), dma((CHUNKS,)),
        dma((CHUNKS,)), dma((CHUNKS,)),
        dma((CHUNKS,)), dma((CHUNKS,)),
        dma((CHUNKS,)), dma((CHUNKS, ring)),
        dma((CHUNKS, ring)), dma((CHUNKS, ring)),
        dma, dma,
    ]
    anywhere = pl.BlockSpec(memory_space=pltpu.HBM)
    vmem = pl.BlockSpec(memory_space=pltpu.VMEM)
    return pl.pallas_call(
        functools.partial(kernel, geometry, scale),
        out_shape=jax.ShapeDtypeStruct(field.shape, BF16),
        in_specs=[anywhere, anywhere, vmem, vmem, anywhere, anywhere, anywhere],
        out_specs=vmem,
        scratch_shapes=scratch,
        compiler_params=pltpu.CompilerParams(
            collective_id=0, has_side_effects=True, vmem_limit_bytes=48 * 1024 * 1024
        ),
        name="spectral_layer",
    )(
        field, spectral_weight, local_weight, bias.reshape(1, channels),
        jnp.asarray(table_z), jnp.asarray(forward), jnp.asarray(back),
    )


def solution(mesh, ring=8, nx=4, nz=8):
    return jax.shard_map(
        functools.partial(on_device, ring, nx, nz),
        mesh=mesh,
        in_specs=(P(None, "gy", None, "gz"), P("gy", None, None, "gz", None), P(), P()),
        out_specs=P(None, "gy", None, "gz"),
        check_vma=False,
    )
```

```python
import functools
import math

import jax
import jax.numpy as jnp
import ml_dtypes
import numpy as np
from jax import lax
from jax.experimental import pallas as pl
from jax.experimental.pallas import tpu as pltpu
from jax.sharding import PartitionSpec as P

MESH = pl.DeviceIdType.MESH
BF16 = jnp.bfloat16
F32 = jnp.float32
CHUNKS = 2
VMEM_BYTES = 48 * 1024 * 1024


def phase_of(number, modulus):
    return (number % modulus).astype(np.float32) * np.float32(2.0 * math.pi / modulus)


def rounded(array):
    return np.asarray(array, np.float32).astype(ml_dtypes.bfloat16).astype(np.float32)


def z_tables(ring, depth):
    size = 2 * ring
    cell = np.arange(depth)
    tables = []
    for d in range(size):
        owner = np.array(
            [((d // 2 + t) % ring) * 2 + (d % 2 ^ r) for r in range(2) for t in range(ring)]
        )
        mode = owner[:, None] * 2 + np.arange(2)
        angle = phase_of(mode[:, :, None] * (cell * size + d), depth * size)
        base = np.stack([np.cos(angle), -np.sin(angle)], 2)
        tables.append(np.repeat(base[:, None], 4, 1).reshape(size * 16, depth))
    return rounded(np.stack(tables))


def y_tables(nx, nz, rows):
    size = nx * nz
    total = rows * size
    forward, back = [], []
    for e in range(size):
        owner = np.array(
            [((e // nz + a) % nx) * nz + (e % nz + b) % nz for a in range(nx) for b in range(nz)]
        )
        mode = owner[:, None] * 2 + np.arange(2)
        wave = np.where(mode < size, mode, mode + total - 2 * size)
        angle = phase_of(wave[:, :, None] * (np.arange(rows) * size + e), total)
        cosine, sine = np.cos(angle), np.sin(angle)
        there = np.stack([np.stack([cosine, sine], -1), np.stack([-sine, cosine], -1)], 2)
        there = np.einsum("ujqyp,kl->ujkqylp", there, np.eye(2))
        forward.append(there.reshape(size * 8, rows * 4))
        here = np.stack([np.stack([cosine, -sine], -1), np.stack([sine, cosine], -1)], 2)
        here = np.einsum("ujqyp,kl->ykqujlp", here, np.eye(2))
        back.append(here.reshape(rows * 4, size * 8))
    return rounded(np.stack(forward)), rounded(np.stack(back))


def gelu_tanh(value):
    return 0.5 * value * (1.0 + jnp.tanh(0.7978845608 * (value + 0.044715 * value * value * value)))


def split(value):
    high = value.astype(BF16)
    return high, (value - high.astype(F32)).astype(BF16)


def dot(left, right, dims=((1,), (0,))):
    return lax.dot_general(left, right, (dims, ((), ())), preferred_element_type=F32)


def kernel(
    geometry, scale,
    field, weight, pointwise_in, bias_in, table_z, table_f, table_b, out,
    fv, wv, pointwise, bias, tz, tf, tb, acc, sib_out, sib_in, a_out, a_in, b_out, b_in, c_in, d_in,
    w_mess, w_out, w_in, w_stage, w_full, small, wide, lin,
    local, local_f, local_w, sib_s, sib_r, a_s, a_r, b_s, b_r, c_s, c_r, d_s, d_r, e_s, e_r, w_s, w_r,
):
    ring, nx, nz, planes, rows, channels, depth = geometry
    gz, gy = 2 * ring, nx * nz
    per = planes // CHUNKS
    lanes = per * channels
    half = lanes // 2
    groups = rows // 4
    band = channels // gz
    d = lax.axis_index("gz")
    e = lax.axis_index("gy")
    core = lax.rem(d, 2)

    def chip(t):
        return {"gz": lax.rem(d + 2 * t, gz)}

    sibling = {"gz": d + 1 - 2 * core}
    ex, ez = e // nz, lax.rem(e, nz)

    def plane(a, b):
        return {"gy": lax.rem(ex + a, nx) * nz + lax.rem(ez + b, nz)}

    partners = [(a, b) for a in range(nx) for b in range(nz)][1:]

    def slot(a, b):
        return ((nx - a) % nx) * nz + (nz - b) % nz

    def remote(src, dst, send, recv, device):
        return pltpu.make_async_remote_copy(
            src_ref=src, dst_ref=dst, send_sem=send, recv_sem=recv, device_id=device, device_id_type=MESH
        )

    get_tz = pltpu.make_async_copy(table_z.at[d], tz, local.at[0])
    get_f = [
        pltpu.make_async_copy(
            field.at[pl.ds(ch * per, per)], fv.at[pl.ds(ch * per, per)], local_f.at[ch]
        )
        for ch in range(CHUNKS)
    ]
    get_w = pltpu.make_async_copy(weight, wv, local.at[1])
    get_tf = pltpu.make_async_copy(table_f.at[e], tf, local.at[2])
    get_tb = pltpu.make_async_copy(table_b.at[e], tb, local.at[3])
    get_tz.start()
    for copy in get_f:
        copy.start()
    get_w.start()
    get_mix = pltpu.make_async_copy(pointwise_in, pointwise, local.at[4])
    get_bias = pltpu.make_async_copy(bias_in, bias, local.at[5])
    get_mix.start()
    get_bias.start()
    get_tf.start()
    get_tb.start()

    barrier = pltpu.get_barrier_semaphore()
    for step in range(1, gz):
        pl.semaphore_signal(
            barrier, inc=1, device_id={"gz": lax.rem(d + step, gz)}, device_id_type=MESH
        )
    for a, b in partners:
        pl.semaphore_signal(barrier, inc=1, device_id=plane(a, b), device_id_type=MESH)

    get_tz.wait()
    member = lax.rem(lax.broadcasted_iota(jnp.int32, (gz * 16, depth), 0) // 4, 4)
    table = jnp.concatenate(
        [jnp.where(member == i, tz[...], 0.0).astype(BF16) for i in range(4)], axis=1
    )
    own_rows = ring * 16

    def cells(ch, g):
        return jnp.concatenate(
            [fv[ch * per : (ch + 1) * per, g * 4 + i].reshape(lanes, depth) for i in range(4)], axis=1
        )

    def to_sibling(ch, g):
        return remote(
            sib_out.at[ch, g], sib_in.at[ch, g], sib_s.at[ch, g], sib_r.at[ch, g], sibling
        )

    def z_sums(ch, g):
        part = dot(table, cells(ch, g), ((1,), (1,)))
        sib_out[ch, g] = part[own_rows:].astype(BF16)
        acc[ch, g] = part[:own_rows]

    get_f[0].wait()
    for g in range(groups):
        z_sums(0, g)
    pl.semaphore_wait(barrier, gz - 1 + gy - 1)
    for g in range(groups):
        to_sibling(0, g).start()

    get_w.wait()
    for jj in range(2):
        for k in range(2 * gz):
            for p in range(2):
                row = (jj * 2 + k % 2) * band
                w_mess[k // 2, row : row + band, p * channels : (p + 1) * channels] = wv[
                    jj, k, p
                ].astype(F32)
    w_out[...] = w_mess[...].astype(BF16)
    own_w = pltpu.make_async_copy(w_out.at[d], w_in.at[d], local_w)
    own_w.start()
    for step in range(1, gz):
        dest = lax.rem(d + step, gz)
        remote(w_out.at[dest], w_in.at[d], w_s, w_r, {"gz": dest}).start()

    for ch in range(1, CHUNKS):
        get_f[ch].wait()
        for g in range(groups):
            z_sums(ch, g)
            to_sibling(ch, g).start()

    def towards(ch, t):
        target, place = {
            1: (1, 0), 7: (7, 1), 2: (2, 2), 6: (6, 3), 3: (1, 4), 5: (7, 5), 4: (6 if ch % 2 else 2, 6)
        }[t]
        return remote(
            a_out.at[ch, t - 1], a_in.at[ch, place], a_s.at[ch], a_r.at[ch, place], chip(target)
        )

    for ch in range(CHUNKS):
        for g in range(groups):
            to_sibling(ch, g).wait_recv()
            total = acc[ch, g] + sib_in[ch, g].astype(F32)
            for t in (0, 2, 6):
                acc[ch, g, t * 16 : (t + 1) * 16] = total[t * 16 : (t + 1) * 16]
            for t in (3, 4, 5, 1, 7):
                a_out[ch, t - 1, g * 16 : (g + 1) * 16] = total[t * 16 : (t + 1) * 16].astype(BF16)
        for t in (3, 5, 4, 1, 7):
            towards(ch, t).start()

    get_mix.wait()
    get_bias.wait()
    block = per * channels
    row_id = lax.broadcasted_iota(jnp.int32, (block, block), 0) // channels
    col_id = lax.broadcasted_iota(jnp.int32, (block, block), 1) // channels
    row = jnp.concatenate([pointwise[...].astype(F32)] * per, axis=1)
    mixing = jnp.where(row_id == col_id, jnp.concatenate([row] * per, axis=0), 0.0).astype(BF16)
    first = lax.broadcasted_iota(jnp.int32, (block, channels), 0)
    second = lax.broadcasted_iota(jnp.int32, (block, channels), 1)
    pick = jnp.where(
        lax.rem(first, channels) == second, jnp.broadcast_to(bias[...].astype(F32), (block, channels)), 0.0
    ).astype(BF16)
    offset = dot(pick, jnp.ones((channels, 4 * depth), BF16))
    def own_sums(ch, t):
        return jnp.concatenate([acc[ch, g, t * 16 : (t + 1) * 16] for g in range(groups)], axis=0)

    for ch in range(CHUNKS):
        for g in range(groups):
            lin[ch, g] = dot(mixing, cells(ch, g)) + offset
        towards(ch, 3).wait_recv()
        towards(ch, 5).wait_recv()
        towards(ch, 4).wait_recv()
        across = a_in[ch, 6].astype(F32)
        right = own_sums(ch, 2) + a_in[ch, 4].astype(F32)
        left = own_sums(ch, 6) + a_in[ch, 5].astype(F32)
        if ch % 2:
            left = left + across
        else:
            right = right + across
        a_out[ch, 1] = right.astype(BF16)
        a_out[ch, 5] = left.astype(BF16)
        towards(ch, 2).start()
        towards(ch, 6).start()

    get_tf.wait()
    ahead = tf[...].astype(BF16)
    ahead = jnp.concatenate([ahead, ahead], axis=1)
    for ch in range(CHUNKS):
        for t in (1, 7, 2, 6):
            towards(ch, t).wait_recv()
        modes = own_sums(ch, 0)
        for place in range(4):
            modes = modes + a_in[ch, place].astype(F32)
        high, low = split(modes)
        part = dot(ahead, jnp.concatenate([high, low], axis=0))
        part = part.reshape(gy, 8, lanes)
        b_out[ch] = jnp.concatenate([part[:, :, :half], part[:, :, half:]], axis=1).astype(BF16)
        b_in[ch, 0] = b_out[ch, 0]
        for a, b in partners:
            remote(
                b_out.at[ch, a * nz + b], b_in.at[ch, slot(a, b)], b_s.at[ch], b_r.at[ch], plane(a, b)
            ).start()

    own_w.wait()
    remote(w_in.at[pl.ds(0, gz - 1)], w_in.at[pl.ds(0, gz - 1)], w_s, w_r, chip(1)).wait_recv()
    w_mess[...] = w_in[...].astype(F32)
    for source in range(gz):
        for jk in range(4):
            w_stage[jk, source * band : (source + 1) * band] = w_mess[
                source, jk * band : (jk + 1) * band
            ]
    sign = jnp.where(
        lax.broadcasted_iota(jnp.int32, (channels, 2 * channels), 1) < channels, -1.0, 1.0
    )
    for jk in range(4):
        upper = w_stage[jk]
        lower = pltpu.roll(upper, channels, 1) * sign
        w_full[jk] = jnp.concatenate([upper, lower], axis=0).astype(BF16)

    per_half = per // 2
    for ch in range(CHUNKS):
        remote(
            b_in.at[ch, pl.ds(1, gy - 1)], b_in.at[ch, pl.ds(1, gy - 1)], b_s.at[ch], b_r.at[ch], plane(0, 1)
        ).wait_recv()
        spectrum = jnp.sum(b_in[ch].astype(F32), axis=0)
        for h in range(half // 128):
            small[h] = spectrum[:, h * 128 : (h + 1) * 128]
        for h in range(half // 128):
            real = small[h, pl.ds(0, 8, stride=2), :]
            imag = small[h, pl.ds(1, 8, stride=2), :]
            for s in range(128 // channels):
                lane = s * channels
                x = h * (128 // channels) + s
                wide[x * 8 : (x + 1) * 8, :] = jnp.concatenate(
                    [real[:, lane : lane + channels], imag[:, lane : lane + channels]], axis=1
                )
        products = []
        for jk in range(4):
            high, low = split(wide[pl.ds(jk, 2 * per_half, stride=4), :])
            both = dot(jnp.concatenate([high, low], axis=0), w_full[jk])
            products.append(both[: 2 * per_half] + both[2 * per_half :])
        for jk in range(4):
            wide[pl.ds(jk, 2 * per_half, stride=4), :] = products[jk]
        for h in range(half // 128):
            pieces = [
                wide[(h * (128 // channels) + s) * 8 : (h * (128 // channels) + s + 1) * 8, :]
                for s in range(128 // channels)
            ]
            small[h, pl.ds(0, 8, stride=2), :] = jnp.concatenate(
                [piece[:, :channels] for piece in pieces], axis=1
            )
            small[h, pl.ds(1, 8, stride=2), :] = jnp.concatenate(
                [piece[:, channels:] for piece in pieces], axis=1
            )
        c_in[ch, 0] = jnp.concatenate([small[h] for h in range(half // 128)], axis=1).astype(BF16)
        for a, b in partners:
            remote(
                c_in.at[ch, 0], c_in.at[ch, slot(a, b)], c_s.at[ch], c_r.at[ch], plane(a, b)
            ).start()

    def gather(ch, t, source=0):
        return remote(
            d_in.at[ch, 0, source], d_in.at[ch, 0, t], d_s.at[ch], d_r.at[ch, t], chip((source - t) % ring)
        )

    def share(ch, t):
        return remote(d_in.at[ch, 0, t], d_in.at[ch, 1, t], e_s.at[ch, t], e_r.at[ch, t], sibling)

    get_tb.wait()
    behind = tb[...].astype(BF16)
    line = lax.broadcasted_iota(jnp.int32, (rows * 4, lanes), 0)
    low_mode = jnp.logical_and(lax.rem(line, 4) < 2, d == 0)
    factor = jnp.where(low_mode, scale, 2.0 * scale)
    for ch in range(CHUNKS):
        remote(
            c_in.at[ch, pl.ds(1, gy - 1)], c_in.at[ch, pl.ds(1, gy - 1)], c_s.at[ch], c_r.at[ch], plane(0, 1)
        ).wait_recv()
        bands = c_in[ch].astype(F32)
        bands = jnp.concatenate([bands[:, 0:8], bands[:, 8:16]], axis=2)
        bands = bands.reshape(gy * 8, lanes).astype(BF16)
        d_in[ch, 0, 0] = (dot(behind, bands) * factor).astype(BF16)
        for t in (6, 2, 7, 1):
            gather(ch, t).start()
        share(ch, 0).start()
    for ch in range(CHUNKS):
        gather(ch, 6).wait_recv()
        gather(ch, 5, 6).start()
        if ch % 2 == 0:
            gather(ch, 4, 6).start()
        gather(ch, 2).wait_recv()
        gather(ch, 3, 2).start()
        if ch % 2:
            gather(ch, 4, 2).start()
        share(ch, 6).start()
        share(ch, 2).start()
        for t in (7, 1):
            gather(ch, t).wait_recv()
            share(ch, t).start()

    for ch in range(CHUNKS):
        for t in (5, 3, 4):
            gather(ch, t).wait_recv()
            share(ch, t).start()
        for t in range(ring):
            share(ch, t).wait_recv()
        for g in range(groups):
            spectral = d_in[ch, :, :, g * 16 : (g + 1) * 16].reshape(gz * 16, lanes)
            value = gelu_tanh(dot(spectral, table, ((0,), (0,))) + lin[ch, g])
            value = value.astype(BF16).reshape(per, channels, 4 * depth)
            for i in range(4):
                out[ch * per : (ch + 1) * per, g * 4 + i] = value[:, :, i * depth : (i + 1) * depth]

    for ch in range(CHUNKS):
        for g in range(groups):
            to_sibling(ch, g).wait_send()
        remote(a_out.at[ch], a_in.at[ch], a_s.at[ch], a_r.at[ch, 0], chip(1)).wait_send()
        remote(
            b_out.at[ch, pl.ds(1, gy - 1)], b_in.at[ch, pl.ds(1, gy - 1)], b_s.at[ch], b_r.at[ch], plane(0, 1)
        ).wait_send()
        remote(
            c_in.at[ch, pl.ds(1, gy - 1)], c_in.at[ch, pl.ds(1, gy - 1)], c_s.at[ch], c_r.at[ch], plane(0, 1)
        ).wait_send()
        remote(
            d_in.at[ch, 0, pl.ds(1, ring - 1)], d_in.at[ch, 0, pl.ds(1, ring - 1)], d_s.at[ch], d_r.at[ch, 1], chip(1)
        ).wait_send()
        for t in range(ring):
            share(ch, t).wait_send()
    remote(w_in.at[pl.ds(0, gz - 1)], w_in.at[pl.ds(0, gz - 1)], w_s, w_r, chip(1)).wait_send()


def on_device(ring, nx, nz, field, spectral_weight, local_weight, bias):
    planes, rows, channels, depth = field.shape
    gz, gy = 2 * ring, nx * nz
    geometry = (ring, nx, nz, planes, rows, channels, depth)
    scale = 1.0 / (rows * gy * depth * gz)
    forward, back = y_tables(nx, nz, rows)
    table_z = z_tables(ring, depth)
    per = planes // CHUNKS
    lanes = per * channels
    half = lanes // 2
    groups = rows // 4
    band = channels // gz
    dma = pltpu.SemaphoreType.DMA
    scratch = [
        pltpu.VMEM(field.shape, BF16),
        pltpu.VMEM(spectral_weight.shape, BF16),
        pltpu.VMEM(local_weight.shape, BF16),
        pltpu.VMEM((1, channels), BF16),
        pltpu.VMEM(table_z.shape[1:], F32),
        pltpu.VMEM(forward.shape[1:], F32),
        pltpu.VMEM(back.shape[1:], F32),
        pltpu.VMEM((CHUNKS, groups, ring * 16, lanes), F32),
        pltpu.VMEM((CHUNKS, groups, ring * 16, lanes), BF16),
        pltpu.VMEM((CHUNKS, groups, ring * 16, lanes), BF16),
        pltpu.VMEM((CHUNKS, ring - 1, rows * 4, lanes), BF16),
        pltpu.VMEM((CHUNKS, ring - 1, rows * 4, lanes), BF16),
        pltpu.VMEM((CHUNKS, gy, 16, half), BF16),
        pltpu.VMEM((CHUNKS, gy, 16, half), BF16),
        pltpu.VMEM((CHUNKS, gy, 16, half), BF16),
        pltpu.VMEM((CHUNKS, 2, ring, rows * 4, lanes), BF16),
        pltpu.VMEM((gz, 4 * band, 2 * channels), F32),
        pltpu.VMEM((gz, 4 * band, 2 * channels), BF16),
        pltpu.VMEM((gz, 4 * band, 2 * channels), BF16),
        pltpu.VMEM((4, channels, 2 * channels), F32),
        pltpu.VMEM((4, 2 * channels, 2 * channels), BF16),
        pltpu.VMEM((half // 128, 16, 128), F32),
        pltpu.VMEM((per * 4, 2 * channels), F32),
        pltpu.VMEM((CHUNKS, groups, lanes, 4 * depth), F32),
        dma((6,)), dma((CHUNKS,)), dma,
        dma((CHUNKS, groups)), dma((CHUNKS, groups)),
        dma((CHUNKS,)), dma((CHUNKS, ring - 1)),
        dma((CHUNKS,)), dma((CHUNKS,)),
        dma((CHUNKS,)), dma((CHUNKS,)),
        dma((CHUNKS,)), dma((CHUNKS, ring)),
        dma((CHUNKS, ring)), dma((CHUNKS, ring)),
        dma, dma,
    ]
    anywhere = pl.BlockSpec(memory_space=pltpu.HBM)
    vmem = pl.BlockSpec(memory_space=pltpu.VMEM)
    return pl.pallas_call(
        functools.partial(kernel, geometry, scale),
        out_shape=pltpu.VMEM(field.shape, BF16),
        in_specs=[anywhere] * 7,
        out_specs=vmem,
        scratch_shapes=scratch,
        compiler_params=pltpu.CompilerParams(
            collective_id=0, has_side_effects=True, vmem_limit_bytes=VMEM_BYTES
        ),
        name="spectral_layer",
    )(
        *[
            pltpu.with_memory_space_constraint(array, pltpu.HBM)
            for array in (
                field, spectral_weight, local_weight, bias.reshape(1, channels),
                jnp.asarray(table_z), jnp.asarray(forward), jnp.asarray(back),
            )
        ]
    )


def solution(mesh, ring=8, nx=4, nz=8):
    return jax.shard_map(
        functools.partial(on_device, ring, nx, nz),
        mesh=mesh,
        in_specs=(P(None, "gy", None, "gz"), P("gy", None, None, "gz", None), P(), P()),
        out_specs=P(None, "gy", None, "gz"),
        check_vma=False,
    )
```

```python
import functools
import math

import jax
import jax.numpy as jnp
import ml_dtypes
import numpy as np
from jax import lax
from jax.experimental import pallas as pl
from jax.experimental.pallas import tpu as pltpu
from jax.sharding import PartitionSpec as P

MESH = pl.DeviceIdType.MESH
BF16 = jnp.bfloat16
F32 = jnp.float32
CHUNKS = 4
ORDER = [
    [("y", 0), ("y", 1), ("y", 2), ("y", 3), ("p", 0), ("p", 1), ("p", 2), ("p", 3)],
    [("l", 0), ("l", 1), ("z", 0), ("l", 2), ("z", 1), ("l", 3), ("z", 2), ("z", 3)],
]
VMEM_BYTES = 48 * 1024 * 1024


def phase_of(number, modulus):
    return (number % modulus).astype(np.float32) * np.float32(2.0 * math.pi / modulus)


def rounded(array):
    return np.asarray(array, np.float32).astype(ml_dtypes.bfloat16).astype(np.float32)


def z_tables(ring, depth):
    size = 2 * ring
    cell = np.arange(depth)
    tables = []
    for d in range(size):
        owner = np.array(
            [((d // 2 + t) % ring) * 2 + (d % 2 ^ r) for r in range(2) for t in range(ring)]
        )
        mode = owner[:, None] * 2 + np.arange(2)
        angle = phase_of(mode[:, :, None] * (cell * size + d), depth * size)
        base = np.stack([np.cos(angle), -np.sin(angle)], 2)
        tables.append(np.repeat(base[:, None], 4, 1).reshape(size * 16, depth))
    return rounded(np.stack(tables))


def y_tables(nx, nz, rows):
    size = nx * nz
    total = rows * size
    forward, back = [], []
    for e in range(size):
        owner = np.array(
            [((e // nz + a) % nx) * nz + (e % nz + b) % nz for a in range(nx) for b in range(nz)]
        )
        mode = owner[:, None] * 2 + np.arange(2)
        wave = np.where(mode < size, mode, mode + total - 2 * size)
        angle = phase_of(wave[:, :, None] * (np.arange(rows) * size + e), total)
        cosine, sine = np.cos(angle), np.sin(angle)
        there = np.stack([np.stack([cosine, sine], -1), np.stack([-sine, cosine], -1)], 2)
        there = np.einsum("ujqyp,kl->ujkqylp", there, np.eye(2))
        forward.append(there.reshape(size * 8, rows * 4))
        here = np.stack([np.stack([cosine, -sine], -1), np.stack([sine, cosine], -1)], 2)
        here = np.einsum("ujqyp,kl->ykqujlp", here, np.eye(2))
        back.append(here.reshape(rows * 4, size * 8))
    return rounded(np.stack(forward)), rounded(np.stack(back))


def gelu_tanh(value):
    return 0.5 * value * (1.0 + jnp.tanh(0.7978845608 * (value + 0.044715 * value * value * value)))


def split(value):
    high = value.astype(BF16)
    return high, (value - high.astype(F32)).astype(BF16)


def dot(left, right, dims=((1,), (0,))):
    return lax.dot_general(left, right, (dims, ((), ())), preferred_element_type=F32)


def kernel(
    geometry, scale,
    field, weight, pointwise_in, bias_in, table_z, table_f, table_b, out,
    fv, wv, pointwise, bias, tz, tf, tb, acc, sib_out, sib_in, a_out, a_in, b_out, b_in, c_in, d_in,
    w_mess, w_out, w_in, w_stage, w_full, small, wide, lin,
    local, local_f, local_w, sib_s, sib_r, a_s, a_r, b_s, b_r, c_s, c_r, d_s, d_r, e_s, e_r, w_s, w_r,
):
    ring, nx, nz, planes, rows, channels, depth = geometry
    gz, gy = 2 * ring, nx * nz
    chunks = range(CHUNKS)
    per = planes // CHUNKS
    lanes = per * channels
    fold = lanes // (2 * channels)
    groups = rows // 4
    band = channels // gz
    d = lax.axis_index("gz")
    e = lax.axis_index("gy")
    core = lax.rem(d, 2)

    def chip(t):
        return {"gz": lax.rem(d + 2 * t, gz)}

    sibling = {"gz": d + 1 - 2 * core}
    ex, ez = e // nz, lax.rem(e, nz)

    def plane(a, b):
        return {"gy": lax.rem(ex + a, nx) * nz + lax.rem(ez + b, nz)}

    partners = sorted(
        [(a, b) for a in range(nx) for b in range(nz)][1:],
        key=lambda step: -min(step[0], nx - step[0]) - min(step[1], nz - step[1]),
    )

    def slot(a, b):
        return ((nx - a) % nx) * nz + (nz - b) % nz

    def remote(src, dst, send, recv, device):
        return pltpu.make_async_remote_copy(
            src_ref=src, dst_ref=dst, send_sem=send, recv_sem=recv, device_id=device, device_id_type=MESH
        )

    def to_sibling(ch):
        return remote(sib_out.at[ch], sib_in.at[ch], sib_s.at[ch], sib_r.at[ch], sibling)

    def towards(ch, t):
        target, place = {
            1: (1, 0), 7: (7, 1), 2: (2, 2), 6: (6, 3), 3: (1, 4), 5: (7, 5), 4: (6 if ch % 2 else 2, 6)
        }[t]
        return remote(
            a_out.at[ch, t - 1], a_in.at[ch, place], a_s.at[ch], a_r.at[ch, place], chip(target)
        )

    def weights_to(step):
        dest = lax.rem(d + step, gz)
        return remote(w_out.at[dest], w_in.at[d], w_s, w_r, {"gz": dest})

    def spread(ch, a, b):
        return remote(
            b_out.at[ch, a * nz + b], b_in.at[ch, slot(a, b)], b_s.at[ch], b_r.at[ch], plane(a, b)
        )

    def all_spread(ch):
        rest = pl.ds(1, gy - 1)
        return remote(b_out.at[ch, rest], b_in.at[ch, rest], b_s.at[ch], b_r.at[ch], plane(0, 1))

    def join(ch, a, b):
        return remote(c_in.at[ch, 0], c_in.at[ch, slot(a, b)], c_s.at[ch], c_r.at[ch], plane(a, b))

    def all_join(ch):
        rest = pl.ds(1, gy - 1)
        return remote(c_in.at[ch, rest], c_in.at[ch, rest], c_s.at[ch], c_r.at[ch], plane(0, 1))

    def gather(ch, t, source=0):
        return remote(
            d_in.at[ch, 0, source], d_in.at[ch, 0, t], d_s.at[ch], d_r.at[ch, t], chip((source - t) % ring)
        )

    def share(ch, t):
        return remote(d_in.at[ch, 0, t], d_in.at[ch, 1, t], e_s.at[ch, t], e_r.at[ch, t], sibling)

    get_tz = pltpu.make_async_copy(table_z.at[d], tz, local.at[0])
    get_f = [
        pltpu.make_async_copy(
            field.at[pl.ds(ch * per, per)], fv.at[pl.ds(ch * per, per)], local_f.at[ch]
        )
        for ch in chunks
    ]
    get_w = pltpu.make_async_copy(weight, wv, local.at[1])
    get_tf = pltpu.make_async_copy(table_f.at[e], tf, local.at[2])
    get_tb = pltpu.make_async_copy(table_b.at[e], tb, local.at[3])
    get_mix = pltpu.make_async_copy(pointwise_in, pointwise, local.at[4])
    get_bias = pltpu.make_async_copy(bias_in, bias, local.at[5])
    get_tz.start()
    for copy in get_f:
        copy.start()
    for copy in (get_w, get_tf, get_tb, get_mix, get_bias):
        copy.start()

    barrier = pltpu.get_barrier_semaphore()
    for step in range(1, gz):
        pl.semaphore_signal(
            barrier, inc=1, device_id={"gz": lax.rem(d + step, gz)}, device_id_type=MESH
        )
    for a, b in partners:
        pl.semaphore_signal(barrier, inc=1, device_id=plane(a, b), device_id_type=MESH)

    get_tz.wait()
    member = lax.rem(lax.broadcasted_iota(jnp.int32, (gz * 16, depth), 0) // 4, 4)
    table = jnp.concatenate(
        [jnp.where(member == i, tz[...], 0.0).astype(BF16) for i in range(4)], axis=1
    )
    own_rows = ring * 16

    def cells(ch, g):
        return jnp.concatenate(
            [fv[ch * per : (ch + 1) * per, g * 4 + i].reshape(lanes, depth) for i in range(4)], axis=1
        )

    for ch in chunks:
        get_f[ch].wait()
        for g in range(groups):
            part = dot(table, cells(ch, g), ((1,), (1,)))
            sib_out[ch, g] = part[own_rows:].astype(BF16)
            acc[ch, g] = part[:own_rows]

    get_w.wait()
    for jj in range(2):
        for k in range(2 * gz):
            for p in range(2):
                row = (jj * 2 + k % 2) * band
                w_mess[k // 2, row : row + band, p * channels : (p + 1) * channels] = wv[
                    jj, k, p
                ].astype(F32)
    w_out[...] = w_mess[...].astype(BF16)
    own_w = pltpu.make_async_copy(w_out.at[d], w_in.at[d], local_w)
    own_w.start()

    pl.semaphore_wait(barrier, gz - 1 + gy - 1)
    for ch in chunks:
        to_sibling(ch).start()
    for step in range(1, gz):
        weights_to(step).start()

    for ch in chunks:
        to_sibling(ch).wait_recv()
        for g in range(groups):
            total = acc[ch, g] + sib_in[ch, g].astype(F32)
            for t in (0, 2, 6):
                acc[ch, g, t * 16 : (t + 1) * 16] = total[t * 16 : (t + 1) * 16]
            for t in (3, 4, 5, 1, 7):
                a_out[ch, t - 1, g * 16 : (g + 1) * 16] = total[t * 16 : (t + 1) * 16].astype(BF16)
        for t in (4, 3, 5):
            towards(ch, t).start()
    for ch in chunks:
        for t in (1, 7):
            towards(ch, t).start()

    get_mix.wait()
    get_bias.wait()
    row_id = lax.broadcasted_iota(jnp.int32, (lanes, lanes), 0) // channels
    col_id = lax.broadcasted_iota(jnp.int32, (lanes, lanes), 1) // channels
    row = jnp.concatenate([pointwise[...].astype(F32)] * per, axis=1)
    mixing = jnp.where(row_id == col_id, jnp.concatenate([row] * per, axis=0), 0.0).astype(BF16)
    first = lax.broadcasted_iota(jnp.int32, (lanes, channels), 0)
    second = lax.broadcasted_iota(jnp.int32, (lanes, channels), 1)
    pick = jnp.where(
        lax.rem(first, channels) == second, jnp.broadcast_to(bias[...].astype(F32), (lanes, channels)), 0.0
    ).astype(BF16)
    offset = dot(pick, jnp.ones((channels, 4 * depth), BF16))
    for ch in chunks:
        for g in range(groups):
            lin[ch, g] = dot(mixing, cells(ch, g)) + offset

    def own_sums(ch, t):
        return jnp.concatenate([acc[ch, g, t * 16 : (t + 1) * 16] for g in range(groups)], axis=0)

    for ch in chunks:
        for t in (3, 5, 4):
            towards(ch, t).wait_recv()
        across = a_in[ch, 6].astype(F32)
        right = own_sums(ch, 2) + a_in[ch, 4].astype(F32)
        left = own_sums(ch, 6) + a_in[ch, 5].astype(F32)
        if ch % 2:
            left = left + across
        else:
            right = right + across
        a_out[ch, 1] = right.astype(BF16)
        a_out[ch, 5] = left.astype(BF16)
        towards(ch, 2).start()
        towards(ch, 6).start()

    get_tf.wait()
    ahead = tf[...].astype(BF16)
    ahead = jnp.concatenate([ahead, ahead], axis=1)
    for ch in chunks:
        for t in (1, 7, 2, 6):
            towards(ch, t).wait_recv()
        modes = own_sums(ch, 0)
        for place in range(4):
            modes = modes + a_in[ch, place].astype(F32)
        high, low = split(modes)
        part = dot(ahead, jnp.concatenate([high, low], axis=0)).reshape(gy, 8, lanes)
        part = jnp.concatenate([part[:, :, h * 128 : (h + 1) * 128] for h in range(fold)], axis=1)
        b_out[ch] = part.astype(BF16)
        b_in[ch, 0] = b_out[ch, 0]
        for a, b in partners:
            spread(ch, a, b).start()

    own_w.wait()
    rest = pl.ds(0, gz - 1)
    remote(w_in.at[rest], w_in.at[rest], w_s, w_r, chip(1)).wait_recv()
    w_mess[...] = w_in[...].astype(F32)
    for source in range(gz):
        for jk in range(4):
            w_stage[jk, source * band : (source + 1) * band] = w_mess[
                source, jk * band : (jk + 1) * band
            ]
    sign = jnp.where(
        lax.broadcasted_iota(jnp.int32, (channels, 2 * channels), 1) < channels, -1.0, 1.0
    )
    for jk in range(4):
        upper = w_stage[jk]
        lower = pltpu.roll(upper, channels, 1) * sign
        w_full[jk] = jnp.concatenate([upper, lower], axis=0).astype(BF16)

    pairs = fold * 4
    for ch in chunks:
        all_spread(ch).wait_recv()
        small[...] = jnp.sum(b_in[ch].astype(F32), axis=0)
        real = small[pl.ds(0, pairs, stride=2), :]
        imag = small[pl.ds(1, pairs, stride=2), :]
        for x in range(2):
            part = slice(x * channels, (x + 1) * channels)
            wide[x * pairs : (x + 1) * pairs, :] = jnp.concatenate([real[:, part], imag[:, part]], axis=1)
        products = []
        for jk in range(4):
            high, low = split(wide[pl.ds(jk, per, stride=4), :])
            both = dot(jnp.concatenate([high.astype(F32), low.astype(F32)], axis=0).astype(BF16), w_full[jk])
            products.append(both[:per] + both[per:])
        for jk in range(4):
            wide[pl.ds(jk, per, stride=4), :] = products[jk]
        pieces = [wide[x * pairs : (x + 1) * pairs, :] for x in range(2)]
        small[pl.ds(0, pairs, stride=2), :] = jnp.concatenate(
            [piece[:, :channels] for piece in pieces], axis=1
        )
        small[pl.ds(1, pairs, stride=2), :] = jnp.concatenate(
            [piece[:, channels:] for piece in pieces], axis=1
        )
        c_in[ch, 0] = small[...].astype(BF16)
        for a, b in partners:
            join(ch, a, b).start()

    get_tb.wait()
    behind = tb[...].astype(BF16)
    line = lax.broadcasted_iota(jnp.int32, (rows * 4, lanes), 0)
    low_mode = jnp.logical_and(lax.rem(line, 4) < 2, d == 0)
    factor = jnp.where(low_mode, scale, 2.0 * scale)

    def back_y(ch):
        all_join(ch).wait_recv()
        bands = c_in[ch].astype(F32)
        bands = jnp.concatenate([bands[:, h * 8 : (h + 1) * 8] for h in range(fold)], axis=2)
        bands = bands.reshape(gy * 8, lanes).astype(BF16)
        d_in[ch, 0, 0] = (dot(behind, bands) * factor).astype(BF16)
        for t in (6, 2):
            gather(ch, t).start()
        share(ch, 0).start()

    def pass_on(ch):
        for t, following in ((6, 5), (2, 3)):
            gather(ch, t).wait_recv()
            gather(ch, following, t).start()
            if t == (2 if ch % 2 else 6):
                gather(ch, 4, t).start()
            share(ch, t).start()
        for t in (7, 1):
            gather(ch, t).start()

    def last_bands(ch):
        for t in (7, 1, 5, 3, 4):
            gather(ch, t).wait_recv()
            share(ch, t).start()

    def back_z(ch):
        for t in range(ring):
            share(ch, t).wait_recv()
        for g in range(groups):
            spectral = d_in[ch, :, :, g * 16 : (g + 1) * 16].reshape(gz * 16, lanes)
            value = gelu_tanh(dot(spectral, table, ((0,), (0,))) + lin[ch, g])
            value = value.astype(BF16).reshape(per, channels, 4 * depth)
            for i in range(4):
                out[ch * per : (ch + 1) * per, g * 4 + i] = value[:, :, i * depth : (i + 1) * depth]

    for step in ORDER:
        for name, ch in step:
            {"y": back_y, "p": pass_on, "l": last_bands, "z": back_z}[name](ch)

    for ch in chunks:
        to_sibling(ch).wait_send()
        remote(a_out.at[ch], a_in.at[ch], a_s.at[ch], a_r.at[ch, 0], chip(1)).wait_send()
        all_spread(ch).wait_send()
        all_join(ch).wait_send()
        others = pl.ds(1, ring - 1)
        remote(
            d_in.at[ch, 0, others], d_in.at[ch, 0, others], d_s.at[ch], d_r.at[ch, 1], chip(1)
        ).wait_send()
        for t in range(ring):
            share(ch, t).wait_send()
    remote(w_in.at[rest], w_in.at[rest], w_s, w_r, chip(1)).wait_send()


def on_device(ring, nx, nz, field, spectral_weight, local_weight, bias):
    planes, rows, channels, depth = field.shape
    gz, gy = 2 * ring, nx * nz
    geometry = (ring, nx, nz, planes, rows, channels, depth)
    scale = 1.0 / (rows * gy * depth * gz)
    forward, back = y_tables(nx, nz, rows)
    table_z = z_tables(ring, depth)
    per = planes // CHUNKS
    lanes = per * channels
    fold = lanes // (2 * channels)
    groups = rows // 4
    band = channels // gz
    dma = pltpu.SemaphoreType.DMA
    scratch = [
        pltpu.VMEM(field.shape, BF16),
        pltpu.VMEM(spectral_weight.shape, BF16),
        pltpu.VMEM(local_weight.shape, BF16),
        pltpu.VMEM((1, channels), BF16),
        pltpu.VMEM(table_z.shape[1:], F32),
        pltpu.VMEM(forward.shape[1:], F32),
        pltpu.VMEM(back.shape[1:], F32),
        pltpu.VMEM((CHUNKS, groups, ring * 16, lanes), F32),
        pltpu.VMEM((CHUNKS, groups, ring * 16, lanes), BF16),
        pltpu.VMEM((CHUNKS, groups, ring * 16, lanes), BF16),
        pltpu.VMEM((CHUNKS, ring - 1, rows * 4, lanes), BF16),
        pltpu.VMEM((CHUNKS, ring - 1, rows * 4, lanes), BF16),
        pltpu.VMEM((CHUNKS, gy, 8 * fold, 2 * channels), BF16),
        pltpu.VMEM((CHUNKS, gy, 8 * fold, 2 * channels), BF16),
        pltpu.VMEM((CHUNKS, gy, 8 * fold, 2 * channels), BF16),
        pltpu.VMEM((CHUNKS, 2, ring, rows * 4, lanes), BF16),
        pltpu.VMEM((gz, 4 * band, 2 * channels), F32),
        pltpu.VMEM((gz, 4 * band, 2 * channels), BF16),
        pltpu.VMEM((gz, 4 * band, 2 * channels), BF16),
        pltpu.VMEM((4, channels, 2 * channels), F32),
        pltpu.VMEM((4, 2 * channels, 2 * channels), BF16),
        pltpu.VMEM((8 * fold, 2 * channels), F32),
        pltpu.VMEM((per * 4, 2 * channels), F32),
        pltpu.VMEM((CHUNKS, groups, lanes, 4 * depth), F32),
        dma((6,)), dma((CHUNKS,)), dma,
        dma((CHUNKS,)), dma((CHUNKS,)),
        dma((CHUNKS,)), dma((CHUNKS, ring - 1)),
        dma((CHUNKS,)), dma((CHUNKS,)),
        dma((CHUNKS,)), dma((CHUNKS,)),
        dma((CHUNKS,)), dma((CHUNKS, ring)),
        dma((CHUNKS, ring)), dma((CHUNKS, ring)),
        dma, dma,
    ]
    anywhere = pl.BlockSpec(memory_space=pltpu.HBM)
    vmem = pl.BlockSpec(memory_space=pltpu.VMEM)
    return pl.pallas_call(
        functools.partial(kernel, geometry, scale),
        out_shape=pltpu.VMEM(field.shape, BF16),
        in_specs=[anywhere] * 7,
        out_specs=vmem,
        scratch_shapes=scratch,
        compiler_params=pltpu.CompilerParams(
            collective_id=0, has_side_effects=True, vmem_limit_bytes=VMEM_BYTES
        ),
        name="spectral_layer",
    )(
        *[
            pltpu.with_memory_space_constraint(array, pltpu.HBM)
            for array in (
                field, spectral_weight, local_weight, bias.reshape(1, channels),
                jnp.asarray(table_z), jnp.asarray(forward), jnp.asarray(back),
            )
        ]
    )


def solution(mesh, ring=8, nx=4, nz=8):
    return jax.shard_map(
        functools.partial(on_device, ring, nx, nz),
        mesh=mesh,
        in_specs=(P(None, "gy", None, "gz"), P("gy", None, None, "gz", None), P(), P()),
        out_specs=P(None, "gy", None, "gz"),
        check_vma=False,
    )
```

```python
import functools
import math

import jax
import jax.numpy as jnp
import ml_dtypes
import numpy as np
from jax import lax
from jax.experimental import pallas as pl
from jax.experimental.pallas import tpu as pltpu
from jax.sharding import PartitionSpec as P

MESH = pl.DeviceIdType.MESH
BF16 = jnp.bfloat16
F32 = jnp.float32
CHUNKS = 4
ORDER = [
    [("y", 0), ("y", 1), ("y", 2), ("y", 3), ("p", 0), ("p", 1), ("p", 2), ("p", 3)],
    [("l", 0), ("l", 1), ("z", 0), ("l", 2), ("z", 1), ("l", 3), ("z", 2), ("z", 3)],
]
VMEM_BYTES = 48 * 1024 * 1024


def phase_of(number, modulus):
    return (number % modulus).astype(np.float32) * np.float32(2.0 * math.pi / modulus)


def rounded(array):
    return np.asarray(array, np.float32).astype(ml_dtypes.bfloat16).astype(np.float32)


def z_tables(ring, depth):
    size = 2 * ring
    cell = np.arange(depth)
    tables = []
    for d in range(size):
        owner = np.array(
            [((d // 2 + t) % ring) * 2 + (d % 2 ^ r) for r in range(2) for t in range(ring)]
        )
        mode = owner[:, None] * 2 + np.arange(2)
        angle = phase_of(mode[:, :, None] * (cell * size + d), depth * size)
        base = np.stack([np.cos(angle), -np.sin(angle)], 2)
        tables.append(np.repeat(base[:, None], 4, 1).reshape(size * 16, depth))
    return rounded(np.stack(tables))


def y_tables(nx, nz, rows):
    size = nx * nz
    total = rows * size
    forward, back = [], []
    for e in range(size):
        owner = np.array(
            [((e // nz + a) % nx) * nz + (e % nz + b) % nz for a in range(nx) for b in range(nz)]
        )
        mode = owner[:, None] * 2 + np.arange(2)
        wave = np.where(mode < size, mode, mode + total - 2 * size)
        angle = phase_of(wave[:, :, None] * (np.arange(rows) * size + e), total)
        cosine, sine = np.cos(angle), np.sin(angle)
        there = np.stack([np.stack([cosine, sine], -1), np.stack([-sine, cosine], -1)], 2)
        there = np.einsum("ujqyp,kl->ujkqylp", there, np.eye(2))
        forward.append(there.reshape(size * 8, rows * 4))
        here = np.stack([np.stack([cosine, -sine], -1), np.stack([sine, cosine], -1)], 2)
        here = np.einsum("ujqyp,kl->ykqujlp", here, np.eye(2))
        back.append(here.reshape(rows * 4, size * 8))
    return rounded(np.stack(forward)), rounded(np.stack(back))


def gelu_tanh(value):
    half = 0.5 * value
    inner = value * (0.7978845608 + (0.7978845608 * 0.044715) * (value * value))
    return half + half * jnp.tanh(inner)


def split(value):
    high = value.astype(BF16)
    return high, (value - high.astype(F32)).astype(BF16)


def dot(left, right, dims=((1,), (0,))):
    return lax.dot_general(left, right, (dims, ((), ())), preferred_element_type=F32)


def kernel(
    geometry, scale,
    field, weight, pointwise_in, bias_in, table_z, table_f, table_b, out,
    fv, wv, pointwise, bias, tz, tf, tb, acc, sib_out, sib_in, a_out, a_in, b_out, b_in, c_in, d_in,
    w_mess, w_out, w_in, w_stage, w_full, small, wide, lin,
    local, local_f, local_w, sib_s, sib_r, a_s, a_r, b_s, b_r, c_s, c_r, d_s, d_r, e_s, e_r, w_s, w_r,
):
    ring, nx, nz, planes, rows, channels, depth = geometry
    gz, gy = 2 * ring, nx * nz
    chunks = range(CHUNKS)
    per = planes // CHUNKS
    lanes = per * channels
    fold = lanes // (2 * channels)
    groups = rows // 4
    band = channels // gz
    d = lax.axis_index("gz")
    e = lax.axis_index("gy")
    core = lax.rem(d, 2)

    def chip(t):
        return {"gz": lax.rem(d + 2 * t, gz)}

    sibling = {"gz": d + 1 - 2 * core}
    ex, ez = e // nz, lax.rem(e, nz)

    def plane(a, b):
        return {"gy": lax.rem(ex + a, nx) * nz + lax.rem(ez + b, nz)}

    partners = sorted(
        [(a, b) for a in range(nx) for b in range(nz)][1:],
        key=lambda step: -min(step[0], nx - step[0]) - min(step[1], nz - step[1]),
    )

    def slot(a, b):
        return ((nx - a) % nx) * nz + (nz - b) % nz

    def remote(src, dst, send, recv, device):
        return pltpu.make_async_remote_copy(
            src_ref=src, dst_ref=dst, send_sem=send, recv_sem=recv, device_id=device, device_id_type=MESH
        )

    def to_sibling(ch):
        return remote(sib_out.at[ch], sib_in.at[ch], sib_s.at[ch], sib_r.at[ch], sibling)

    def towards(ch, t):
        target, place = {
            1: (1, 0), 7: (7, 1), 2: (2, 2), 6: (6, 3), 3: (1, 4), 5: (7, 5), 4: (6 if ch % 2 else 2, 6)
        }[t]
        return remote(
            a_out.at[ch, t - 1], a_in.at[ch, place], a_s.at[ch], a_r.at[ch, place], chip(target)
        )

    def weights_to(step):
        dest = lax.rem(d + step, gz)
        return remote(w_out.at[dest], w_in.at[d], w_s, w_r, {"gz": dest})

    def spread(ch, a, b):
        return remote(
            b_out.at[ch, a * nz + b], b_in.at[ch, slot(a, b)], b_s.at[ch], b_r.at[ch], plane(a, b)
        )

    def all_spread(ch):
        rest = pl.ds(1, gy - 1)
        return remote(b_out.at[ch, rest], b_in.at[ch, rest], b_s.at[ch], b_r.at[ch], plane(0, 1))

    def join(ch, a, b):
        return remote(c_in.at[ch, 0], c_in.at[ch, slot(a, b)], c_s.at[ch], c_r.at[ch], plane(a, b))

    def all_join(ch):
        rest = pl.ds(1, gy - 1)
        return remote(c_in.at[ch, rest], c_in.at[ch, rest], c_s.at[ch], c_r.at[ch], plane(0, 1))

    def gather(ch, t, source=0):
        return remote(
            d_in.at[ch, 0, source], d_in.at[ch, 0, t], d_s.at[ch], d_r.at[ch, t], chip((source - t) % ring)
        )

    def share(ch, t):
        return remote(d_in.at[ch, 0, t], d_in.at[ch, 1, t], e_s.at[ch, t], e_r.at[ch, t], sibling)

    barrier = pltpu.get_barrier_semaphore()
    for a, b in partners:
        pl.semaphore_signal(barrier, inc=1, device_id=plane(a, b), device_id_type=MESH)
    for step in range(1, gz):
        pl.semaphore_signal(
            barrier, inc=1, device_id={"gz": lax.rem(d + step, gz)}, device_id_type=MESH
        )

    get_tz = pltpu.make_async_copy(table_z.at[d], tz, local.at[0])
    get_f = [
        pltpu.make_async_copy(
            field.at[pl.ds(ch * per, per)], fv.at[pl.ds(ch * per, per)], local_f.at[ch]
        )
        for ch in chunks
    ]
    get_w = pltpu.make_async_copy(weight, wv, local.at[1])
    get_tf = pltpu.make_async_copy(table_f.at[e], tf, local.at[2])
    get_tb = pltpu.make_async_copy(table_b.at[e], tb, local.at[3])
    get_mix = pltpu.make_async_copy(pointwise_in, pointwise, local.at[4])
    get_bias = pltpu.make_async_copy(bias_in, bias, local.at[5])
    get_tz.start()
    for copy in get_f:
        copy.start()
    for copy in (get_w, get_tf, get_tb, get_mix, get_bias):
        copy.start()

    get_tz.wait()
    member = lax.rem(lax.broadcasted_iota(jnp.int32, (gz * 16, depth), 0) // 4, 4)
    table = jnp.concatenate(
        [jnp.where(member == i, tz[...], 0.0).astype(BF16) for i in range(4)], axis=1
    )
    own_rows = ring * 16

    def cells(ch, g):
        return jnp.concatenate(
            [fv[ch * per : (ch + 2) * per, g * 4 + i].reshape(2 * lanes, depth) for i in range(4)], axis=1
        )

    for ch in chunks[::2]:
        get_f[ch].wait()
        get_f[ch + 1].wait()
        for g in range(groups):
            part = dot(table, cells(ch, g), ((1,), (1,)))
            for side in range(2):
                mine = part[:, side * lanes : (side + 1) * lanes]
                sib_out[ch + side, g] = mine[own_rows:].astype(BF16)
                acc[ch + side, g] = mine[:own_rows]

    get_w.wait()
    for jj in range(2):
        for k in range(2 * gz):
            for p in range(2):
                row = (jj * 2 + k % 2) * band
                w_mess[k // 2, row : row + band, p * channels : (p + 1) * channels] = wv[
                    jj, k, p
                ].astype(F32)
    w_out[...] = w_mess[...].astype(BF16)
    own_w = pltpu.make_async_copy(w_out.at[d], w_in.at[d], local_w)
    own_w.start()

    pl.semaphore_wait(barrier, gz - 1 + gy - 1)
    for ch in chunks:
        to_sibling(ch).start()
    for step in range(1, gz):
        weights_to(step).start()

    for ch in chunks:
        to_sibling(ch).wait_recv()
        for g in range(groups):
            total = acc[ch, g] + sib_in[ch, g].astype(F32)
            for t in (0, 2, 6):
                acc[ch, g, t * 16 : (t + 1) * 16] = total[t * 16 : (t + 1) * 16]
            for t in (3, 4, 5, 1, 7):
                a_out[ch, t - 1, g * 16 : (g + 1) * 16] = total[t * 16 : (t + 1) * 16].astype(BF16)
        for t in (4, 3, 5):
            towards(ch, t).start()
    for ch in chunks:
        for t in (1, 7):
            towards(ch, t).start()

    get_mix.wait()
    get_bias.wait()
    row_id = lax.broadcasted_iota(jnp.int32, (2 * lanes, 2 * lanes), 0) // channels
    col_id = lax.broadcasted_iota(jnp.int32, (2 * lanes, 2 * lanes), 1) // channels
    row = jnp.concatenate([pointwise[...].astype(F32)] * (2 * per), axis=1)
    mixing = jnp.where(row_id == col_id, jnp.concatenate([row] * (2 * per), axis=0), 0.0).astype(BF16)
    first = lax.broadcasted_iota(jnp.int32, (2 * lanes, channels), 0)
    second = lax.broadcasted_iota(jnp.int32, (2 * lanes, channels), 1)
    pick = jnp.where(
        lax.rem(first, channels) == second, jnp.broadcast_to(bias[...].astype(F32), (2 * lanes, channels)), 0.0
    ).astype(BF16)
    offset = dot(pick, jnp.ones((channels, 4 * depth), BF16))
    for ch in chunks[::2]:
        for g in range(groups):
            mapped = dot(mixing, cells(ch, g)) + offset
            lin[ch, g] = mapped[:lanes]
            lin[ch + 1, g] = mapped[lanes:]

    def own_sums(ch, t):
        return jnp.concatenate([acc[ch, g, t * 16 : (t + 1) * 16] for g in range(groups)], axis=0)

    for ch in chunks:
        for t in (3, 5, 4):
            towards(ch, t).wait_recv()
        across = a_in[ch, 6].astype(F32)
        right = own_sums(ch, 2) + a_in[ch, 4].astype(F32)
        left = own_sums(ch, 6) + a_in[ch, 5].astype(F32)
        if ch % 2:
            left = left + across
        else:
            right = right + across
        a_out[ch, 1] = right.astype(BF16)
        a_out[ch, 5] = left.astype(BF16)
        towards(ch, 2).start()
        towards(ch, 6).start()

    get_tf.wait()
    ahead = tf[...].astype(BF16)
    ahead = jnp.concatenate([ahead, ahead], axis=1)
    for ch in chunks:
        for t in (1, 7, 2, 6):
            towards(ch, t).wait_recv()
        modes = own_sums(ch, 0)
        for place in range(4):
            modes = modes + a_in[ch, place].astype(F32)
        high, low = split(modes)
        part = dot(ahead, jnp.concatenate([high, low], axis=0)).reshape(gy, 8, lanes)
        part = jnp.concatenate([part[:, :, h * 128 : (h + 1) * 128] for h in range(fold)], axis=1)
        b_out[ch] = part.astype(BF16)
        b_in[ch, 0] = b_out[ch, 0]
        for a, b in partners:
            spread(ch, a, b).start()

    own_w.wait()
    rest = pl.ds(0, gz - 1)
    remote(w_in.at[rest], w_in.at[rest], w_s, w_r, chip(1)).wait_recv()
    w_mess[...] = w_in[...].astype(F32)
    for source in range(gz):
        for jk in range(4):
            w_stage[jk, source * band : (source + 1) * band] = w_mess[
                source, jk * band : (jk + 1) * band
            ]
    sign = jnp.where(
        lax.broadcasted_iota(jnp.int32, (channels, 2 * channels), 1) < channels, -1.0, 1.0
    )
    for jk in range(4):
        upper = w_stage[jk]
        lower = pltpu.roll(upper, channels, 1) * sign
        w_full[jk] = jnp.concatenate([upper, lower], axis=0).astype(BF16)

    pairs = fold * 4
    for ch in chunks:
        all_spread(ch).wait_recv()
        small[...] = jnp.sum(b_in[ch].astype(F32), axis=0)
        real = small[pl.ds(0, pairs, stride=2), :]
        imag = small[pl.ds(1, pairs, stride=2), :]
        for x in range(2):
            part = slice(x * channels, (x + 1) * channels)
            wide[x * pairs : (x + 1) * pairs, :] = jnp.concatenate([real[:, part], imag[:, part]], axis=1)
        products = []
        for jk in range(4):
            high, low = split(wide[pl.ds(jk, per, stride=4), :])
            both = dot(jnp.concatenate([high.astype(F32), low.astype(F32)], axis=0).astype(BF16), w_full[jk])
            products.append(both[:per] + both[per:])
        for jk in range(4):
            wide[pl.ds(jk, per, stride=4), :] = products[jk]
        pieces = [wide[x * pairs : (x + 1) * pairs, :] for x in range(2)]
        small[pl.ds(0, pairs, stride=2), :] = jnp.concatenate(
            [piece[:, :channels] for piece in pieces], axis=1
        )
        small[pl.ds(1, pairs, stride=2), :] = jnp.concatenate(
            [piece[:, channels:] for piece in pieces], axis=1
        )
        c_in[ch, 0] = small[...].astype(BF16)
        for a, b in partners:
            join(ch, a, b).start()

    get_tb.wait()
    behind = tb[...].astype(BF16)
    line = lax.broadcasted_iota(jnp.int32, (rows * 4, lanes), 0)
    low_mode = jnp.logical_and(lax.rem(line, 4) < 2, d == 0)
    factor = jnp.where(low_mode, scale, 2.0 * scale)

    def back_y(ch):
        all_join(ch).wait_recv()
        bands = c_in[ch].astype(F32)
        bands = jnp.concatenate([bands[:, h * 8 : (h + 1) * 8] for h in range(fold)], axis=2)
        bands = bands.reshape(gy * 8, lanes).astype(BF16)
        d_in[ch, 0, 0] = (dot(behind, bands) * factor).astype(BF16)
        for t in (6, 2):
            gather(ch, t).start()
        share(ch, 0).start()

    def pass_on(ch):
        for t, following in ((6, 5), (2, 3)):
            gather(ch, t).wait_recv()
            gather(ch, following, t).start()
            if t == (2 if ch % 2 else 6):
                gather(ch, 4, t).start()
            share(ch, t).start()
        for t in (7, 1):
            gather(ch, t).start()

    def last_bands(ch):
        for t in (7, 1, 5, 3, 4):
            gather(ch, t).wait_recv()
            share(ch, t).start()

    def back_z(ch):
        for t in range(ring):
            share(ch, t).wait_recv()
        for g in range(groups):
            spectral = d_in[ch, :, :, g * 16 : (g + 1) * 16].reshape(gz * 16, lanes)
            value = gelu_tanh(dot(spectral, table, ((0,), (0,))) + lin[ch, g])
            value = value.astype(BF16).reshape(per, channels, 4 * depth)
            for i in range(4):
                out[ch * per : (ch + 1) * per, g * 4 + i] = value[:, :, i * depth : (i + 1) * depth]

    for step in ORDER:
        for name, ch in step:
            {"y": back_y, "p": pass_on, "l": last_bands, "z": back_z}[name](ch)

    for ch in chunks:
        to_sibling(ch).wait_send()
        remote(a_out.at[ch], a_in.at[ch], a_s.at[ch], a_r.at[ch, 0], chip(1)).wait_send()
        all_spread(ch).wait_send()
        all_join(ch).wait_send()
        others = pl.ds(1, ring - 1)
        remote(
            d_in.at[ch, 0, others], d_in.at[ch, 0, others], d_s.at[ch], d_r.at[ch, 1], chip(1)
        ).wait_send()
        for t in range(ring):
            share(ch, t).wait_send()
    remote(w_in.at[rest], w_in.at[rest], w_s, w_r, chip(1)).wait_send()


def on_device(ring, nx, nz, field, spectral_weight, local_weight, bias):
    planes, rows, channels, depth = field.shape
    gz, gy = 2 * ring, nx * nz
    geometry = (ring, nx, nz, planes, rows, channels, depth)
    scale = 1.0 / (rows * gy * depth * gz)
    forward, back = y_tables(nx, nz, rows)
    table_z = z_tables(ring, depth)
    per = planes // CHUNKS
    lanes = per * channels
    fold = lanes // (2 * channels)
    groups = rows // 4
    band = channels // gz
    dma = pltpu.SemaphoreType.DMA
    scratch = [
        pltpu.VMEM(field.shape, BF16),
        pltpu.VMEM(spectral_weight.shape, BF16),
        pltpu.VMEM(local_weight.shape, BF16),
        pltpu.VMEM((1, channels), BF16),
        pltpu.VMEM(table_z.shape[1:], F32),
        pltpu.VMEM(forward.shape[1:], F32),
        pltpu.VMEM(back.shape[1:], F32),
        pltpu.VMEM((CHUNKS, groups, ring * 16, lanes), F32),
        pltpu.VMEM((CHUNKS, groups, ring * 16, lanes), BF16),
        pltpu.VMEM((CHUNKS, groups, ring * 16, lanes), BF16),
        pltpu.VMEM((CHUNKS, ring - 1, rows * 4, lanes), BF16),
        pltpu.VMEM((CHUNKS, ring - 1, rows * 4, lanes), BF16),
        pltpu.VMEM((CHUNKS, gy, 8 * fold, 2 * channels), BF16),
        pltpu.VMEM((CHUNKS, gy, 8 * fold, 2 * channels), BF16),
        pltpu.VMEM((CHUNKS, gy, 8 * fold, 2 * channels), BF16),
        pltpu.VMEM((CHUNKS, 2, ring, rows * 4, lanes), BF16),
        pltpu.VMEM((gz, 4 * band, 2 * channels), F32),
        pltpu.VMEM((gz, 4 * band, 2 * channels), BF16),
        pltpu.VMEM((gz, 4 * band, 2 * channels), BF16),
        pltpu.VMEM((4, channels, 2 * channels), F32),
        pltpu.VMEM((4, 2 * channels, 2 * channels), BF16),
        pltpu.VMEM((8 * fold, 2 * channels), F32),
        pltpu.VMEM((per * 4, 2 * channels), F32),
        pltpu.VMEM((CHUNKS, groups, lanes, 4 * depth), F32),
        dma((6,)), dma((CHUNKS,)), dma,
        dma((CHUNKS,)), dma((CHUNKS,)),
        dma((CHUNKS,)), dma((CHUNKS, ring - 1)),
        dma((CHUNKS,)), dma((CHUNKS,)),
        dma((CHUNKS,)), dma((CHUNKS,)),
        dma((CHUNKS,)), dma((CHUNKS, ring)),
        dma((CHUNKS, ring)), dma((CHUNKS, ring)),
        dma, dma,
    ]
    anywhere = pl.BlockSpec(memory_space=pltpu.HBM)
    vmem = pl.BlockSpec(memory_space=pltpu.VMEM)
    return pl.pallas_call(
        functools.partial(kernel, geometry, scale),
        out_shape=pltpu.VMEM(field.shape, BF16),
        in_specs=[anywhere] * 7,
        out_specs=vmem,
        scratch_shapes=scratch,
        compiler_params=pltpu.CompilerParams(
            collective_id=0, has_side_effects=True, vmem_limit_bytes=VMEM_BYTES
        ),
        name="spectral_layer",
    )(
        *[
            pltpu.with_memory_space_constraint(array, pltpu.HBM)
            for array in (
                field, spectral_weight, local_weight, bias.reshape(1, channels),
                jnp.asarray(table_z), jnp.asarray(forward), jnp.asarray(back),
            )
        ]
    )


def solution(mesh, ring=8, nx=4, nz=8):
    return jax.shard_map(
        functools.partial(on_device, ring, nx, nz),
        mesh=mesh,
        in_specs=(P(None, "gy", None, "gz"), P("gy", None, None, "gz", None), P(), P()),
        out_specs=P(None, "gy", None, "gz"),
        check_vma=False,
    )
```

```python
import functools
import math

import jax
import jax.numpy as jnp
import ml_dtypes
import numpy as np
from jax import lax
from jax.experimental import pallas as pl
from jax.experimental.pallas import tpu as pltpu
from jax.sharding import PartitionSpec as P

MESH = pl.DeviceIdType.MESH
BF16 = jnp.bfloat16
F32 = jnp.float32
CHUNKS = 4
ORDER = [
    [("y", 0), ("y", 1), ("y", 2), ("y", 3), ("p", 0), ("p", 1), ("p", 2), ("p", 3)],
    [("l", 0), ("l", 1), ("z", 0), ("l", 2), ("z", 1), ("l", 3), ("z", 2), ("z", 3)],
]
VMEM_BYTES = 48 * 1024 * 1024


def phase_of(number, modulus):
    return (number % modulus).astype(np.float32) * np.float32(2.0 * math.pi / modulus)


def rounded(array):
    return np.asarray(array, np.float32).astype(ml_dtypes.bfloat16).astype(np.float32)


def z_tables(ring, depth):
    size = 2 * ring
    cell = np.arange(depth)
    tables = []
    for d in range(size):
        owner = np.array(
            [((d // 2 + t) % ring) * 2 + (d % 2 ^ r) for r in range(2) for t in range(ring)]
        )
        mode = owner[:, None] * 2 + np.arange(2)
        angle = phase_of(mode[:, :, None] * (cell * size + d), depth * size)
        base = np.stack([np.cos(angle), -np.sin(angle)], 2)
        tables.append(np.repeat(base[:, None], 4, 1).reshape(size * 16, depth))
    return rounded(np.stack(tables))


def y_tables(nx, nz, rows):
    size = nx * nz
    total = rows * size
    forward, back = [], []
    for e in range(size):
        owner = np.array(
            [((e // nz + a) % nx) * nz + (e % nz + b) % nz for a in range(nx) for b in range(nz)]
        )
        mode = owner[:, None] * 2 + np.arange(2)
        wave = np.where(mode < size, mode, mode + total - 2 * size)
        angle = phase_of(wave[:, :, None] * (np.arange(rows) * size + e), total)
        cosine, sine = np.cos(angle), np.sin(angle)
        there = np.stack([np.stack([cosine, sine], -1), np.stack([-sine, cosine], -1)], 2)
        there = np.einsum("ujqyp,kl->ujkqylp", there, np.eye(2))
        forward.append(there.reshape(size * 8, rows * 4))
        here = np.stack([np.stack([cosine, -sine], -1), np.stack([sine, cosine], -1)], 2)
        here = np.einsum("ujqyp,kl->ykqujlp", here, np.eye(2))
        back.append(here.reshape(rows * 4, size * 8))
    return rounded(np.stack(forward)), rounded(np.stack(back))


def gelu_tanh(value):
    half = 0.5 * value
    inner = value * (0.7978845608 + (0.7978845608 * 0.044715) * (value * value))
    return half + half * jnp.tanh(inner)


def split(value):
    high = value.astype(BF16)
    return high, (value - high.astype(F32)).astype(BF16)


def dot(left, right, dims=((1,), (0,))):
    return lax.dot_general(left, right, (dims, ((), ())), preferred_element_type=F32)


def kernel(
    geometry, scale,
    field, weight, pointwise_in, bias_in, table_z, table_f, table_b, out,
    fv, wv, pointwise, bias, tz, tf, tb, acc, sib_out, sib_in, a_out, a_in, b_out, b_in, c_in, d_in,
    w_mess, w_out, w_in, w_stage, w_full, small, wide, lin,
    local, local_f, local_w, sib_s, sib_r, a_s, a_r, b_s, b_r, c_s, c_r, d_s, d_r, e_s, e_r, w_s, w_r,
):
    ring, nx, nz, planes, rows, channels, depth = geometry
    gz, gy = 2 * ring, nx * nz
    chunks = range(CHUNKS)
    per = planes // CHUNKS
    lanes = per * channels
    fold = lanes // (2 * channels)
    groups = rows // 4
    band = channels // gz
    d = lax.axis_index("gz")
    e = lax.axis_index("gy")
    core = lax.rem(d, 2)

    def chip(t):
        return {"gz": lax.rem(d + 2 * t, gz)}

    sibling = {"gz": d + 1 - 2 * core}
    ex, ez = e // nz, lax.rem(e, nz)

    def plane(a, b):
        return {"gy": lax.rem(ex + a, nx) * nz + lax.rem(ez + b, nz)}

    partners = sorted(
        [(a, b) for a in range(nx) for b in range(nz)][1:],
        key=lambda step: -min(step[0], nx - step[0]) - min(step[1], nz - step[1]),
    )

    def slot(a, b):
        return ((nx - a) % nx) * nz + (nz - b) % nz

    def remote(src, dst, send, recv, device):
        return pltpu.make_async_remote_copy(
            src_ref=src, dst_ref=dst, send_sem=send, recv_sem=recv, device_id=device, device_id_type=MESH
        )

    def to_sibling(ch):
        return remote(sib_out.at[ch], sib_in.at[ch], sib_s.at[ch], sib_r.at[ch], sibling)

    def towards(ch, t):
        target, place = {
            1: (1, 0), 7: (7, 1), 2: (2, 2), 6: (6, 3), 3: (1, 4), 5: (7, 5), 4: (6 if ch % 2 else 2, 6)
        }[t]
        return remote(
            a_out.at[ch, t - 1], a_in.at[ch, place], a_s.at[ch], a_r.at[ch, place], chip(target)
        )

    def weights_to(step):
        dest = lax.rem(d + step, gz)
        return remote(w_out.at[dest], w_in.at[d], w_s, w_r, {"gz": dest})

    def spread(ch, a, b):
        return remote(
            b_out.at[ch, a * nz + b], b_in.at[ch, slot(a, b)], b_s.at[ch], b_r.at[ch], plane(a, b)
        )

    def all_spread(ch):
        rest = pl.ds(1, gy - 1)
        return remote(b_out.at[ch, rest], b_in.at[ch, rest], b_s.at[ch], b_r.at[ch], plane(0, 1))

    def join(ch, a, b):
        return remote(c_in.at[ch, 0], c_in.at[ch, slot(a, b)], c_s.at[ch], c_r.at[ch], plane(a, b))

    def all_join(ch):
        rest = pl.ds(1, gy - 1)
        return remote(c_in.at[ch, rest], c_in.at[ch, rest], c_s.at[ch], c_r.at[ch], plane(0, 1))

    def gather(ch, t, source=0):
        return remote(
            d_in.at[ch, 0, source], d_in.at[ch, 0, t], d_s.at[ch], d_r.at[ch, t], chip((source - t) % ring)
        )

    def share(ch, part):
        bands = (pl.ds(0, 3), pl.ds(6, 2), pl.ds(3, 3))[part]
        return remote(
            d_in.at[ch, 0, bands], d_in.at[ch, 1, bands], e_s.at[ch, part], e_r.at[ch, part], sibling
        )

    barrier = pltpu.get_barrier_semaphore()
    for a, b in partners:
        pl.semaphore_signal(barrier, inc=1, device_id=plane(a, b), device_id_type=MESH)
    for step in range(1, gz):
        pl.semaphore_signal(
            barrier, inc=1, device_id={"gz": lax.rem(d + step, gz)}, device_id_type=MESH
        )

    get_tz = pltpu.make_async_copy(table_z.at[d], tz, local.at[0])
    get_f = [
        pltpu.make_async_copy(
            field.at[pl.ds(ch * per, per)], fv.at[pl.ds(ch * per, per)], local_f.at[ch]
        )
        for ch in chunks
    ]
    get_w = pltpu.make_async_copy(weight, wv, local.at[1])
    get_tf = pltpu.make_async_copy(table_f.at[e], tf, local.at[2])
    get_tb = pltpu.make_async_copy(table_b.at[e], tb, local.at[3])
    get_mix = pltpu.make_async_copy(pointwise_in, pointwise, local.at[4])
    get_bias = pltpu.make_async_copy(bias_in, bias, local.at[5])
    get_tz.start()
    for copy in get_f:
        copy.start()
    for copy in (get_w, get_tf, get_tb, get_mix, get_bias):
        copy.start()

    get_tz.wait()
    member = lax.rem(lax.broadcasted_iota(jnp.int32, (gz * 16, depth), 0) // 4, 4)
    table = jnp.concatenate(
        [jnp.where(member == i, tz[...], 0.0).astype(BF16) for i in range(4)], axis=1
    )
    own_rows = ring * 16

    def cells(ch, g):
        return jnp.concatenate(
            [fv[ch * per : (ch + 2) * per, g * 4 + i].reshape(2 * lanes, depth) for i in range(4)], axis=1
        )

    for ch in chunks[::2]:
        get_f[ch].wait()
        get_f[ch + 1].wait()
        for g in range(groups):
            part = dot(table, cells(ch, g), ((1,), (1,)))
            for side in range(2):
                mine = part[:, side * lanes : (side + 1) * lanes]
                sib_out[ch + side, g] = mine[own_rows:].astype(BF16)
                acc[ch + side, g] = mine[:own_rows]

    get_w.wait()
    for jj in range(2):
        for k in range(2 * gz):
            for p in range(2):
                row = (jj * 2 + k % 2) * band
                w_mess[k // 2, row : row + band, p * channels : (p + 1) * channels] = wv[
                    jj, k, p
                ].astype(F32)
    w_out[...] = w_mess[...].astype(BF16)
    own_w = pltpu.make_async_copy(w_out.at[d], w_in.at[d], local_w)
    own_w.start()

    pl.semaphore_wait(barrier, gz - 1 + gy - 1)
    for ch in chunks:
        to_sibling(ch).start()
    for step in range(1, gz):
        weights_to(step).start()

    for ch in chunks:
        to_sibling(ch).wait_recv()
        for g in range(groups):
            total = acc[ch, g] + sib_in[ch, g].astype(F32)
            for t in (0, 2, 6):
                acc[ch, g, t * 16 : (t + 1) * 16] = total[t * 16 : (t + 1) * 16]
            for t in (3, 4, 5, 1, 7):
                a_out[ch, t - 1, g * 16 : (g + 1) * 16] = total[t * 16 : (t + 1) * 16].astype(BF16)
        for t in (4, 3, 5):
            towards(ch, t).start()
    for ch in chunks:
        for t in (1, 7):
            towards(ch, t).start()

    get_mix.wait()
    get_bias.wait()
    row_id = lax.broadcasted_iota(jnp.int32, (2 * lanes, 2 * lanes), 0) // channels
    col_id = lax.broadcasted_iota(jnp.int32, (2 * lanes, 2 * lanes), 1) // channels
    row = jnp.concatenate([pointwise[...].astype(F32)] * (2 * per), axis=1)
    mixing = jnp.where(row_id == col_id, jnp.concatenate([row] * (2 * per), axis=0), 0.0).astype(BF16)
    first = lax.broadcasted_iota(jnp.int32, (2 * lanes, channels), 0)
    second = lax.broadcasted_iota(jnp.int32, (2 * lanes, channels), 1)
    pick = jnp.where(
        lax.rem(first, channels) == second, jnp.broadcast_to(bias[...].astype(F32), (2 * lanes, channels)), 0.0
    ).astype(BF16)
    offset = dot(pick, jnp.ones((channels, 4 * depth), BF16))
    for ch in chunks[::2]:
        for g in range(groups):
            mapped = dot(mixing, cells(ch, g)) + offset
            lin[ch, g] = mapped[:lanes]
            lin[ch + 1, g] = mapped[lanes:]

    def own_sums(ch, t):
        return jnp.concatenate([acc[ch, g, t * 16 : (t + 1) * 16] for g in range(groups)], axis=0)

    for ch in chunks:
        for t in (3, 5, 4):
            towards(ch, t).wait_recv()
        across = a_in[ch, 6].astype(F32)
        right = own_sums(ch, 2) + a_in[ch, 4].astype(F32)
        left = own_sums(ch, 6) + a_in[ch, 5].astype(F32)
        if ch % 2:
            left = left + across
        else:
            right = right + across
        a_out[ch, 1] = right.astype(BF16)
        a_out[ch, 5] = left.astype(BF16)
        towards(ch, 2).start()
        towards(ch, 6).start()

    get_tf.wait()
    ahead = tf[...].astype(BF16)
    ahead = jnp.concatenate([ahead, ahead], axis=1)
    for ch in chunks:
        for t in (1, 7, 2, 6):
            towards(ch, t).wait_recv()
        modes = own_sums(ch, 0)
        for place in range(4):
            modes = modes + a_in[ch, place].astype(F32)
        high, low = split(modes)
        part = dot(ahead, jnp.concatenate([high, low], axis=0)).reshape(gy, 8, lanes)
        part = jnp.concatenate([part[:, :, h * 128 : (h + 1) * 128] for h in range(fold)], axis=1)
        b_out[ch] = part.astype(BF16)
        b_in[ch, 0] = b_out[ch, 0]
        for a, b in partners:
            spread(ch, a, b).start()

    own_w.wait()
    rest = pl.ds(0, gz - 1)
    remote(w_in.at[rest], w_in.at[rest], w_s, w_r, chip(1)).wait_recv()
    w_mess[...] = w_in[...].astype(F32)
    for source in range(gz):
        for jk in range(4):
            w_stage[jk, source * band : (source + 1) * band] = w_mess[
                source, jk * band : (jk + 1) * band
            ]
    sign = jnp.where(
        lax.broadcasted_iota(jnp.int32, (channels, 2 * channels), 1) < channels, -1.0, 1.0
    )
    for jk in range(4):
        upper = w_stage[jk]
        lower = pltpu.roll(upper, channels, 1) * sign
        w_full[jk] = jnp.concatenate([upper, lower], axis=0).astype(BF16)

    pairs = fold * 4
    for ch in chunks:
        all_spread(ch).wait_recv()
        small[...] = jnp.sum(b_in[ch].astype(F32), axis=0)
        real = small[pl.ds(0, pairs, stride=2), :]
        imag = small[pl.ds(1, pairs, stride=2), :]
        for x in range(2):
            part = slice(x * channels, (x + 1) * channels)
            wide[x * pairs : (x + 1) * pairs, :] = jnp.concatenate([real[:, part], imag[:, part]], axis=1)
        products = []
        for jk in range(4):
            high, low = split(wide[pl.ds(jk, per, stride=4), :])
            both = dot(jnp.concatenate([high.astype(F32), low.astype(F32)], axis=0).astype(BF16), w_full[jk])
            products.append(both[:per] + both[per:])
        for jk in range(4):
            wide[pl.ds(jk, per, stride=4), :] = products[jk]
        pieces = [wide[x * pairs : (x + 1) * pairs, :] for x in range(2)]
        small[pl.ds(0, pairs, stride=2), :] = jnp.concatenate(
            [piece[:, :channels] for piece in pieces], axis=1
        )
        small[pl.ds(1, pairs, stride=2), :] = jnp.concatenate(
            [piece[:, channels:] for piece in pieces], axis=1
        )
        c_in[ch, 0] = small[...].astype(BF16)
        for a, b in partners:
            join(ch, a, b).start()

    get_tb.wait()
    behind = tb[...].astype(BF16)
    line = lax.broadcasted_iota(jnp.int32, (rows * 4, lanes), 0)
    low_mode = jnp.logical_and(lax.rem(line, 4) < 2, d == 0)
    factor = jnp.where(low_mode, scale, 2.0 * scale)

    def back_y(ch):
        all_join(ch).wait_recv()
        bands = c_in[ch].astype(F32)
        bands = jnp.concatenate([bands[:, h * 8 : (h + 1) * 8] for h in range(fold)], axis=2)
        bands = bands.reshape(gy * 8, lanes).astype(BF16)
        d_in[ch, 0, 0] = (dot(behind, bands) * factor).astype(BF16)
        for t in (6, 2, 7, 1):
            gather(ch, t).start()

    def pass_on(ch):
        for t, following in ((6, 5), (2, 3)):
            gather(ch, t).wait_recv()
            gather(ch, following, t).start()
            if t == (2 if ch % 2 else 6):
                gather(ch, 4, t).start()
    def last_bands(ch):
        for t in (7, 1):
            gather(ch, t).wait_recv()
        share(ch, 0).start()
        share(ch, 1).start()
        for t in (5, 3, 4):
            gather(ch, t).wait_recv()
        share(ch, 2).start()

    def back_z(ch):
        for part in range(3):
            share(ch, part).wait_recv()
        for g in range(groups):
            spectral = d_in[ch, :, :, g * 16 : (g + 1) * 16].reshape(gz * 16, lanes)
            value = gelu_tanh(dot(spectral, table, ((0,), (0,))) + lin[ch, g])
            value = value.astype(BF16).reshape(per, channels, 4 * depth)
            for i in range(4):
                out[ch * per : (ch + 1) * per, g * 4 + i] = value[:, :, i * depth : (i + 1) * depth]

    for step in ORDER:
        for name, ch in step:
            {"y": back_y, "p": pass_on, "l": last_bands, "z": back_z}[name](ch)

    for ch in chunks:
        to_sibling(ch).wait_send()
        remote(a_out.at[ch], a_in.at[ch], a_s.at[ch], a_r.at[ch, 0], chip(1)).wait_send()
        all_spread(ch).wait_send()
        all_join(ch).wait_send()
        others = pl.ds(1, ring - 1)
        remote(
            d_in.at[ch, 0, others], d_in.at[ch, 0, others], d_s.at[ch], d_r.at[ch, 1], chip(1)
        ).wait_send()
        for part in range(3):
            share(ch, part).wait_send()
    remote(w_in.at[rest], w_in.at[rest], w_s, w_r, chip(1)).wait_send()


def on_device(ring, nx, nz, field, spectral_weight, local_weight, bias):
    planes, rows, channels, depth = field.shape
    gz, gy = 2 * ring, nx * nz
    geometry = (ring, nx, nz, planes, rows, channels, depth)
    scale = 1.0 / (rows * gy * depth * gz)
    forward, back = y_tables(nx, nz, rows)
    table_z = z_tables(ring, depth)
    per = planes // CHUNKS
    lanes = per * channels
    fold = lanes // (2 * channels)
    groups = rows // 4
    band = channels // gz
    dma = pltpu.SemaphoreType.DMA
    scratch = [
        pltpu.VMEM(field.shape, BF16),
        pltpu.VMEM(spectral_weight.shape, BF16),
        pltpu.VMEM(local_weight.shape, BF16),
        pltpu.VMEM((1, channels), BF16),
        pltpu.VMEM(table_z.shape[1:], F32),
        pltpu.VMEM(forward.shape[1:], F32),
        pltpu.VMEM(back.shape[1:], F32),
        pltpu.VMEM((CHUNKS, groups, ring * 16, lanes), F32),
        pltpu.VMEM((CHUNKS, groups, ring * 16, lanes), BF16),
        pltpu.VMEM((CHUNKS, groups, ring * 16, lanes), BF16),
        pltpu.VMEM((CHUNKS, ring - 1, rows * 4, lanes), BF16),
        pltpu.VMEM((CHUNKS, ring - 1, rows * 4, lanes), BF16),
        pltpu.VMEM((CHUNKS, gy, 8 * fold, 2 * channels), BF16),
        pltpu.VMEM((CHUNKS, gy, 8 * fold, 2 * channels), BF16),
        pltpu.VMEM((CHUNKS, gy, 8 * fold, 2 * channels), BF16),
        pltpu.VMEM((CHUNKS, 2, ring, rows * 4, lanes), BF16),
        pltpu.VMEM((gz, 4 * band, 2 * channels), F32),
        pltpu.VMEM((gz, 4 * band, 2 * channels), BF16),
        pltpu.VMEM((gz, 4 * band, 2 * channels), BF16),
        pltpu.VMEM((4, channels, 2 * channels), F32),
        pltpu.VMEM((4, 2 * channels, 2 * channels), BF16),
        pltpu.VMEM((8 * fold, 2 * channels), F32),
        pltpu.VMEM((per * 4, 2 * channels), F32),
        pltpu.VMEM((CHUNKS, groups, lanes, 4 * depth), F32),
        dma((6,)), dma((CHUNKS,)), dma,
        dma((CHUNKS,)), dma((CHUNKS,)),
        dma((CHUNKS,)), dma((CHUNKS, ring - 1)),
        dma((CHUNKS,)), dma((CHUNKS,)),
        dma((CHUNKS,)), dma((CHUNKS,)),
        dma((CHUNKS,)), dma((CHUNKS, ring)),
        dma((CHUNKS, 3)), dma((CHUNKS, 3)),
        dma, dma,
    ]
    anywhere = pl.BlockSpec(memory_space=pltpu.HBM)
    vmem = pl.BlockSpec(memory_space=pltpu.VMEM)
    return pl.pallas_call(
        functools.partial(kernel, geometry, scale),
        out_shape=pltpu.VMEM(field.shape, BF16),
        in_specs=[anywhere] * 7,
        out_specs=vmem,
        scratch_shapes=scratch,
        compiler_params=pltpu.CompilerParams(
            collective_id=0, has_side_effects=True, vmem_limit_bytes=VMEM_BYTES
        ),
        name="spectral_layer",
    )(
        *[
            pltpu.with_memory_space_constraint(array, pltpu.HBM)
            for array in (
                field, spectral_weight, local_weight, bias.reshape(1, channels),
                jnp.asarray(table_z), jnp.asarray(forward), jnp.asarray(back),
            )
        ]
    )


def solution(mesh, ring=8, nx=4, nz=8):
    return jax.shard_map(
        functools.partial(on_device, ring, nx, nz),
        mesh=mesh,
        in_specs=(P(None, "gy", None, "gz"), P("gy", None, None, "gz", None), P(), P()),
        out_specs=P(None, "gy", None, "gz"),
        check_vma=False,
    )
```

```python
import functools
import math

import jax
import jax.numpy as jnp
import ml_dtypes
import numpy as np
from jax import lax
from jax.experimental import pallas as pl
from jax.experimental.pallas import tpu as pltpu
from jax.sharding import PartitionSpec as P

MESH = pl.DeviceIdType.MESH
BF16 = jnp.bfloat16
F32 = jnp.float32
CHUNKS = 4
ORDER = [
    [("y", 0), ("y", 1), ("y", 2), ("y", 3), ("p", 0), ("p", 1), ("p", 2), ("p", 3)],
    [("l", 0), ("l", 1), ("z", 0), ("l", 2), ("z", 1), ("l", 3), ("z", 2), ("z", 3)],
]
VMEM_BYTES = 48 * 1024 * 1024


def phase_of(number, modulus):
    return (number % modulus).astype(np.float32) * np.float32(2.0 * math.pi / modulus)


def rounded(array):
    return np.asarray(array, np.float32).astype(ml_dtypes.bfloat16).astype(np.float32)


def z_tables(ring, depth):
    size = 2 * ring
    cell = np.arange(depth)
    tables = []
    for d in range(size):
        owner = np.array(
            [((d // 2 + t) % ring) * 2 + (d % 2 ^ r) for r in range(2) for t in range(ring)]
        )
        mode = owner[:, None] * 2 + np.arange(2)
        angle = phase_of(mode[:, :, None] * (cell * size + d), depth * size)
        base = np.stack([np.cos(angle), -np.sin(angle)], 2)
        tables.append(np.repeat(base[:, None], 4, 1).reshape(size * 16, depth))
    return rounded(np.stack(tables))


def y_tables(nx, nz, rows):
    size = nx * nz
    total = rows * size
    forward, back = [], []
    for e in range(size):
        owner = np.array(
            [((e // nz + a) % nx) * nz + (e % nz + b) % nz for a in range(nx) for b in range(nz)]
        )
        mode = owner[:, None] * 2 + np.arange(2)
        wave = np.where(mode < size, mode, mode + total - 2 * size)
        angle = phase_of(wave[:, :, None] * (np.arange(rows) * size + e), total)
        cosine, sine = np.cos(angle), np.sin(angle)
        there = np.stack([np.stack([cosine, sine], -1), np.stack([-sine, cosine], -1)], 2)
        there = np.einsum("ujqyp,kl->ujkqylp", there, np.eye(2))
        forward.append(there.reshape(size * 8, rows * 4))
        here = np.stack([np.stack([cosine, -sine], -1), np.stack([sine, cosine], -1)], 2)
        here = np.einsum("ujqyp,kl->ykqujlp", here, np.eye(2))
        back.append(here.reshape(rows * 4, size * 8))
    return rounded(np.stack(forward)), rounded(np.stack(back))


def gelu_tanh(value):
    half = 0.5 * value
    inner = value * (0.7978845608 + (0.7978845608 * 0.044715) * (value * value))
    return half + half * jnp.tanh(inner)


def split(value):
    high = value.astype(BF16)
    return high, (value - high.astype(F32)).astype(BF16)


def dot(left, right, dims=((1,), (0,))):
    return lax.dot_general(left, right, (dims, ((), ())), preferred_element_type=F32)


def kernel(
    geometry, scale,
    field, weight, pointwise_in, bias_in, table_z, table_f, table_b, out,
    fv, wv, pointwise, bias, tz, tf, tb, acc, sib_out, sib_in, a_out, a_in, b_out, b_in, c_in, d_in,
    w_mess, w_out, w_in, w_stage, w_full, small, wide, lin,
    local, local_f, local_w, sib_s, sib_r, a_s, a_r, b_s, b_r, c_s, c_r, d_s, d_r, e_s, e_r, w_s, w_r,
):
    ring, nx, nz, planes, rows, channels, depth = geometry
    gz, gy = 2 * ring, nx * nz
    chunks = range(CHUNKS)
    per = planes // CHUNKS
    lanes = per * channels
    fold = lanes // (2 * channels)
    groups = rows // 4
    band = channels // gz
    d = lax.axis_index("gz")
    e = lax.axis_index("gy")
    core = lax.rem(d, 2)

    def chip(t):
        return {"gz": lax.rem(d + 2 * t, gz)}

    sibling = {"gz": d + 1 - 2 * core}
    ex, ez = e // nz, lax.rem(e, nz)

    def plane(a, b):
        return {"gy": lax.rem(ex + a, nx) * nz + lax.rem(ez + b, nz)}

    partners = sorted(
        [(a, b) for a in range(nx) for b in range(nz)][1:],
        key=lambda step: -min(step[0], nx - step[0]) - min(step[1], nz - step[1]),
    )

    def slot(a, b):
        return ((nx - a) % nx) * nz + (nz - b) % nz

    def remote(src, dst, send, recv, device):
        return pltpu.make_async_remote_copy(
            src_ref=src, dst_ref=dst, send_sem=send, recv_sem=recv, device_id=device, device_id_type=MESH
        )

    def to_sibling(ch):
        return remote(sib_out.at[ch], sib_in.at[ch], sib_s.at[ch], sib_r.at[ch], sibling)

    place_of = {3: 0, 1: 1, 5: 2, 7: 3, 4: 4, 2: 5, 6: 6}

    def towards(ch, t):
        target = {3: 1, 5: 7, 4: 6 if ch % 2 else 2, 2: 2, 6: 6}[t]
        place = place_of[t]
        blocks = pl.ds(place, 2 if t in (3, 5) else 1)
        return remote(
            a_out.at[ch, blocks], a_in.at[ch, blocks], a_s.at[ch], a_r.at[ch, place], chip(target)
        )

    def weights_to(step):
        dest = lax.rem(d + step, gz)
        return remote(w_out.at[dest], w_in.at[d], w_s, w_r, {"gz": dest})

    def spread(ch, a, b):
        return remote(
            b_out.at[ch, a * nz + b], b_in.at[ch, slot(a, b)], b_s.at[ch], b_r.at[ch], plane(a, b)
        )

    def all_spread(ch):
        rest = pl.ds(1, gy - 1)
        return remote(b_out.at[ch, rest], b_in.at[ch, rest], b_s.at[ch], b_r.at[ch], plane(0, 1))

    def join(ch, a, b):
        return remote(c_in.at[ch, 0], c_in.at[ch, slot(a, b)], c_s.at[ch], c_r.at[ch], plane(a, b))

    def all_join(ch):
        rest = pl.ds(1, gy - 1)
        return remote(c_in.at[ch, rest], c_in.at[ch, rest], c_s.at[ch], c_r.at[ch], plane(0, 1))

    def gather(ch, t, source=0):
        return remote(
            d_in.at[ch, 0, source], d_in.at[ch, 0, t], d_s.at[ch], d_r.at[ch, t], chip((source - t) % ring)
        )

    def share(ch, part):
        bands = (pl.ds(0, 3), pl.ds(6, 2), pl.ds(3, 3))[part]
        return remote(
            d_in.at[ch, 0, bands], d_in.at[ch, 1, bands], e_s.at[ch, part], e_r.at[ch, part], sibling
        )

    barrier = pltpu.get_barrier_semaphore()
    for a, b in partners:
        pl.semaphore_signal(barrier, inc=1, device_id=plane(a, b), device_id_type=MESH)
    for step in range(1, gz):
        pl.semaphore_signal(
            barrier, inc=1, device_id={"gz": lax.rem(d + step, gz)}, device_id_type=MESH
        )

    get_tz = pltpu.make_async_copy(table_z.at[d], tz, local.at[0])
    get_f = [
        pltpu.make_async_copy(
            field.at[pl.ds(ch * per, per)], fv.at[pl.ds(ch * per, per)], local_f.at[ch]
        )
        for ch in chunks
    ]
    get_w = pltpu.make_async_copy(weight, wv, local.at[1])
    get_tf = pltpu.make_async_copy(table_f.at[e], tf, local.at[2])
    get_tb = pltpu.make_async_copy(table_b.at[e], tb, local.at[3])
    get_mix = pltpu.make_async_copy(pointwise_in, pointwise, local.at[4])
    get_bias = pltpu.make_async_copy(bias_in, bias, local.at[5])
    get_tz.start()
    for copy in get_f:
        copy.start()
    for copy in (get_w, get_tf, get_tb, get_mix, get_bias):
        copy.start()

    get_tz.wait()
    member = lax.rem(lax.broadcasted_iota(jnp.int32, (gz * 16, depth), 0) // 4, 4)
    table = jnp.concatenate(
        [jnp.where(member == i, tz[...], 0.0).astype(BF16) for i in range(4)], axis=1
    )
    own_rows = ring * 16

    def cells(ch, g):
        return jnp.concatenate(
            [fv[ch * per : (ch + 2) * per, g * 4 + i].reshape(2 * lanes, depth) for i in range(4)], axis=1
        )

    for ch in chunks[::2]:
        get_f[ch].wait()
        get_f[ch + 1].wait()
        for g in range(groups):
            part = dot(table, cells(ch, g), ((1,), (1,)))
            for side in range(2):
                mine = part[:, side * lanes : (side + 1) * lanes]
                sib_out[ch + side, g] = mine[own_rows:].astype(BF16)
                acc[ch + side, g] = mine[:own_rows]

    get_w.wait()
    for jj in range(2):
        for k in range(2 * gz):
            for p in range(2):
                row = (jj * 2 + k % 2) * band
                w_mess[k // 2, row : row + band, p * channels : (p + 1) * channels] = wv[
                    jj, k, p
                ].astype(F32)
    w_out[...] = w_mess[...].astype(BF16)
    own_w = pltpu.make_async_copy(w_out.at[d], w_in.at[d], local_w)
    own_w.start()

    pl.semaphore_wait(barrier, gz - 1 + gy - 1)
    for ch in chunks:
        to_sibling(ch).start()
    for step in range(1, gz):
        weights_to(step).start()

    for ch in chunks:
        to_sibling(ch).wait_recv()
        for g in range(groups):
            total = acc[ch, g] + sib_in[ch, g].astype(F32)
            for t in (0, 2, 6):
                acc[ch, g, t * 16 : (t + 1) * 16] = total[t * 16 : (t + 1) * 16]
            for t in (3, 4, 5, 1, 7):
                a_out[ch, place_of[t], g * 16 : (g + 1) * 16] = total[t * 16 : (t + 1) * 16].astype(BF16)
        for t in (4, 3, 5):
            towards(ch, t).start()

    get_mix.wait()
    get_bias.wait()
    row_id = lax.broadcasted_iota(jnp.int32, (2 * lanes, 2 * lanes), 0) // channels
    col_id = lax.broadcasted_iota(jnp.int32, (2 * lanes, 2 * lanes), 1) // channels
    row = jnp.concatenate([pointwise[...].astype(F32)] * (2 * per), axis=1)
    mixing = jnp.where(row_id == col_id, jnp.concatenate([row] * (2 * per), axis=0), 0.0).astype(BF16)
    first = lax.broadcasted_iota(jnp.int32, (2 * lanes, channels), 0)
    second = lax.broadcasted_iota(jnp.int32, (2 * lanes, channels), 1)
    pick = jnp.where(
        lax.rem(first, channels) == second, jnp.broadcast_to(bias[...].astype(F32), (2 * lanes, channels)), 0.0
    ).astype(BF16)
    offset = dot(pick, jnp.ones((channels, 4 * depth), BF16))
    for ch in chunks[::2]:
        for g in range(groups):
            mapped = dot(mixing, cells(ch, g)) + offset
            lin[ch, g] = mapped[:lanes]
            lin[ch + 1, g] = mapped[lanes:]

    def own_sums(ch, t):
        return jnp.concatenate([acc[ch, g, t * 16 : (t + 1) * 16] for g in range(groups)], axis=0)

    for ch in chunks:
        for t in (3, 5, 4):
            towards(ch, t).wait_recv()
        across = a_in[ch, place_of[4]].astype(F32)
        right = own_sums(ch, 2) + a_in[ch, place_of[3]].astype(F32)
        left = own_sums(ch, 6) + a_in[ch, place_of[5]].astype(F32)
        if ch % 2:
            left = left + across
        else:
            right = right + across
        a_out[ch, place_of[2]] = right.astype(BF16)
        a_out[ch, place_of[6]] = left.astype(BF16)
        towards(ch, 2).start()
        towards(ch, 6).start()

    get_tf.wait()
    ahead = tf[...].astype(BF16)
    ahead = jnp.concatenate([ahead, ahead], axis=1)
    for ch in chunks:
        for t in (2, 6):
            towards(ch, t).wait_recv()
        modes = own_sums(ch, 0)
        for t in (1, 7, 2, 6):
            modes = modes + a_in[ch, place_of[t]].astype(F32)
        high, low = split(modes)
        part = dot(ahead, jnp.concatenate([high, low], axis=0)).reshape(gy, 8, lanes)
        part = jnp.concatenate([part[:, :, h * 128 : (h + 1) * 128] for h in range(fold)], axis=1)
        b_out[ch] = part.astype(BF16)
        b_in[ch, 0] = b_out[ch, 0]
        for a, b in partners:
            spread(ch, a, b).start()

    own_w.wait()
    rest = pl.ds(0, gz - 1)
    remote(w_in.at[rest], w_in.at[rest], w_s, w_r, chip(1)).wait_recv()
    w_mess[...] = w_in[...].astype(F32)
    for source in range(gz):
        for jk in range(4):
            w_stage[jk, source * band : (source + 1) * band] = w_mess[
                source, jk * band : (jk + 1) * band
            ]
    sign = jnp.where(
        lax.broadcasted_iota(jnp.int32, (channels, 2 * channels), 1) < channels, -1.0, 1.0
    )
    for jk in range(4):
        upper = w_stage[jk]
        lower = pltpu.roll(upper, channels, 1) * sign
        w_full[jk] = jnp.concatenate([upper, lower], axis=0).astype(BF16)

    pairs = fold * 4
    for ch in chunks:
        all_spread(ch).wait_recv()
        small[...] = jnp.sum(b_in[ch].astype(F32), axis=0)
        real = small[pl.ds(0, pairs, stride=2), :]
        imag = small[pl.ds(1, pairs, stride=2), :]
        for x in range(2):
            part = slice(x * channels, (x + 1) * channels)
            wide[x * pairs : (x + 1) * pairs, :] = jnp.concatenate([real[:, part], imag[:, part]], axis=1)
        products = []
        for jk in range(4):
            high, low = split(wide[pl.ds(jk, per, stride=4), :])
            both = dot(jnp.concatenate([high.astype(F32), low.astype(F32)], axis=0).astype(BF16), w_full[jk])
            products.append(both[:per] + both[per:])
        for jk in range(4):
            wide[pl.ds(jk, per, stride=4), :] = products[jk]
        pieces = [wide[x * pairs : (x + 1) * pairs, :] for x in range(2)]
        small[pl.ds(0, pairs, stride=2), :] = jnp.concatenate(
            [piece[:, :channels] for piece in pieces], axis=1
        )
        small[pl.ds(1, pairs, stride=2), :] = jnp.concatenate(
            [piece[:, channels:] for piece in pieces], axis=1
        )
        c_in[ch, 0] = small[...].astype(BF16)
        for a, b in partners:
            join(ch, a, b).start()

    get_tb.wait()
    behind = tb[...].astype(BF16)
    line = lax.broadcasted_iota(jnp.int32, (rows * 4, lanes), 0)
    low_mode = jnp.logical_and(lax.rem(line, 4) < 2, d == 0)
    factor = jnp.where(low_mode, scale, 2.0 * scale)

    def back_y(ch):
        all_join(ch).wait_recv()
        bands = c_in[ch].astype(F32)
        bands = jnp.concatenate([bands[:, h * 8 : (h + 1) * 8] for h in range(fold)], axis=2)
        bands = bands.reshape(gy * 8, lanes).astype(BF16)
        d_in[ch, 0, 0] = (dot(behind, bands) * factor).astype(BF16)
        for t in (6, 2, 7, 1):
            gather(ch, t).start()

    def pass_on(ch):
        for t, following in ((6, 5), (2, 3)):
            gather(ch, t).wait_recv()
            gather(ch, following, t).start()
            if t == (2 if ch % 2 else 6):
                gather(ch, 4, t).start()
    def last_bands(ch):
        for t in (7, 1):
            gather(ch, t).wait_recv()
        share(ch, 0).start()
        share(ch, 1).start()
        for t in (5, 3, 4):
            gather(ch, t).wait_recv()
        share(ch, 2).start()

    def back_z(ch):
        for part in range(3):
            share(ch, part).wait_recv()
        for g in range(groups):
            spectral = d_in[ch, :, :, g * 16 : (g + 1) * 16].reshape(gz * 16, lanes)
            value = gelu_tanh(dot(spectral, table, ((0,), (0,))) + lin[ch, g])
            value = value.astype(BF16).reshape(per, channels, 4 * depth)
            for i in range(4):
                out[ch * per : (ch + 1) * per, g * 4 + i] = value[:, :, i * depth : (i + 1) * depth]

    for step in ORDER:
        for name, ch in step:
            {"y": back_y, "p": pass_on, "l": last_bands, "z": back_z}[name](ch)

    for ch in chunks:
        to_sibling(ch).wait_send()
        remote(a_out.at[ch], a_in.at[ch], a_s.at[ch], a_r.at[ch, 0], chip(1)).wait_send()
        all_spread(ch).wait_send()
        all_join(ch).wait_send()
        others = pl.ds(1, ring - 1)
        remote(
            d_in.at[ch, 0, others], d_in.at[ch, 0, others], d_s.at[ch], d_r.at[ch, 1], chip(1)
        ).wait_send()
        for part in range(3):
            share(ch, part).wait_send()
    remote(w_in.at[rest], w_in.at[rest], w_s, w_r, chip(1)).wait_send()


def on_device(ring, nx, nz, field, spectral_weight, local_weight, bias):
    planes, rows, channels, depth = field.shape
    gz, gy = 2 * ring, nx * nz
    geometry = (ring, nx, nz, planes, rows, channels, depth)
    scale = 1.0 / (rows * gy * depth * gz)
    forward, back = y_tables(nx, nz, rows)
    table_z = z_tables(ring, depth)
    per = planes // CHUNKS
    lanes = per * channels
    fold = lanes // (2 * channels)
    groups = rows // 4
    band = channels // gz
    dma = pltpu.SemaphoreType.DMA
    scratch = [
        pltpu.VMEM(field.shape, BF16),
        pltpu.VMEM(spectral_weight.shape, BF16),
        pltpu.VMEM(local_weight.shape, BF16),
        pltpu.VMEM((1, channels), BF16),
        pltpu.VMEM(table_z.shape[1:], F32),
        pltpu.VMEM(forward.shape[1:], F32),
        pltpu.VMEM(back.shape[1:], F32),
        pltpu.VMEM((CHUNKS, groups, ring * 16, lanes), F32),
        pltpu.VMEM((CHUNKS, groups, ring * 16, lanes), BF16),
        pltpu.VMEM((CHUNKS, groups, ring * 16, lanes), BF16),
        pltpu.VMEM((CHUNKS, ring - 1, rows * 4, lanes), BF16),
        pltpu.VMEM((CHUNKS, ring - 1, rows * 4, lanes), BF16),
        pltpu.VMEM((CHUNKS, gy, 8 * fold, 2 * channels), BF16),
        pltpu.VMEM((CHUNKS, gy, 8 * fold, 2 * channels), BF16),
        pltpu.VMEM((CHUNKS, gy, 8 * fold, 2 * channels), BF16),
        pltpu.VMEM((CHUNKS, 2, ring, rows * 4, lanes), BF16),
        pltpu.VMEM((gz, 4 * band, 2 * channels), F32),
        pltpu.VMEM((gz, 4 * band, 2 * channels), BF16),
        pltpu.VMEM((gz, 4 * band, 2 * channels), BF16),
        pltpu.VMEM((4, channels, 2 * channels), F32),
        pltpu.VMEM((4, 2 * channels, 2 * channels), BF16),
        pltpu.VMEM((8 * fold, 2 * channels), F32),
        pltpu.VMEM((per * 4, 2 * channels), F32),
        pltpu.VMEM((CHUNKS, groups, lanes, 4 * depth), F32),
        dma((6,)), dma((CHUNKS,)), dma,
        dma((CHUNKS,)), dma((CHUNKS,)),
        dma((CHUNKS,)), dma((CHUNKS, ring - 1)),
        dma((CHUNKS,)), dma((CHUNKS,)),
        dma((CHUNKS,)), dma((CHUNKS,)),
        dma((CHUNKS,)), dma((CHUNKS, ring)),
        dma((CHUNKS, 3)), dma((CHUNKS, 3)),
        dma, dma,
    ]
    anywhere = pl.BlockSpec(memory_space=pltpu.HBM)
    vmem = pl.BlockSpec(memory_space=pltpu.VMEM)
    return pl.pallas_call(
        functools.partial(kernel, geometry, scale),
        out_shape=pltpu.VMEM(field.shape, BF16),
        in_specs=[anywhere] * 7,
        out_specs=vmem,
        scratch_shapes=scratch,
        compiler_params=pltpu.CompilerParams(
            collective_id=0, has_side_effects=True, vmem_limit_bytes=VMEM_BYTES
        ),
        name="spectral_layer",
    )(
        *[
            pltpu.with_memory_space_constraint(array, pltpu.HBM)
            for array in (
                field, spectral_weight, local_weight, bias.reshape(1, channels),
                jnp.asarray(table_z), jnp.asarray(forward), jnp.asarray(back),
            )
        ]
    )


def solution(mesh, ring=8, nx=4, nz=8):
    return jax.shard_map(
        functools.partial(on_device, ring, nx, nz),
        mesh=mesh,
        in_specs=(P(None, "gy", None, "gz"), P("gy", None, None, "gz", None), P(), P()),
        out_specs=P(None, "gy", None, "gz"),
        check_vma=False,
    )
```
